256 devices in a mesh: lev: 4 (over y), tile: 64 (over x, z, core).
Axes of the slice: x: 4, y: 4, z: 8, core: 2. Of those that a mesh axis runs over, the one named last changes fastest.
Arguments:
- atm_state: bfloat16 [12, 6, 524288], P('lev', None, 'tile'), may hold values from -6 to 6
- surface: bfloat16 [4, 524288], P('lev', 'tile'), may hold values from -6 to 6
- mlp_in: bfloat16 [76, 512], replicated, may hold values from -0.625 to 0.625
- mlp_mid: bfloat16 [512, 512], replicated, may hold values from -0.25 to 0.25
- mlp_out: bfloat16 [512, 72], replicated, may hold values from -0.25 to 0.25
- mlp_flux: bfloat16 [512, 8], replicated, may hold values from -0.25 to 0.25
- ocean_state: bfloat16 [76, 1024, 512], P(None, 'tile', 'lev'), may hold values from -6 to 6
- ocean_mask: int32 [1024, 512], P('tile', 'lev'), may hold values 0 or 1
- fold_map: int32 [1024], replicated, may hold values from 0 to 1023, as said below
- pair_tile: int32 [64, 4, 4], P('tile', 'lev'), may hold values from 0 to 63
- pair_block: int32 [64, 4, 4], P('tile', 'lev'), may hold values from 0 to 15
- pair_count: int32 [64, 4], P('tile', 'lev'), may hold values from 1 to 4, as said below
- margin: bfloat16 [4, 128, 1024, 512], P(None, None, 'tile', 'lev'), may hold values from 0.00049 to 1
- conv_in: bfloat16 [3, 3, 84, 256], replicated, may hold values from -0.21875 to 0.21875
- conv_mid: bfloat16 [3, 3, 256, 256], replicated, may hold values from -0.125 to 0.125
- conv_out: bfloat16 [3, 3, 256, 76], replicated, may hold values from -0.125 to 0.125
Outputs:
- atm_next: bfloat16 [12, 6, 524288], P('lev', None, 'tile')
- ocean_next: bfloat16 [76, 1024, 512], P(None, 'tile', 'lev')
The draws below stay inside these ranges and needn't reach their ends.
Inputs may be any that keep to these rules, and one draw needn't show every extreme that they name: The fold reflects the columns about a seam: fold_map[x] = (s - 1 - x) mod 1024 for every column x, with one offset s of 0 to 1023 for the whole grid. `pair_tile`: the source of a slot is the atmosphere block of the device with the same lev index and this tile index. `pair_count`: slots at and beyond the count hold entries that are not used.
All inputs are finite; a program needn't handle non-finite values. No bound on the sum of `ocean_mask` on one device may be relied on, other than what follows from the above.
Results may differ from the reference program's by a relative error of at most 0.0055.
Values may be sent and summed in bfloat16 or wider, within the bound.
No kernel may reach another device: no remote copies, remote signals or barrier semaphores. Data moves between devices by JAX's collectives and lax.ppermute only.
A program may use at most 128 MiB of HBM per device.

```python
import math
import jax
import jax.numpy as jnp
from jax import lax

FIELDS = 6
HID = 512
FLUX = 8
BLK = 128
PAIRS = 4
CH = 256
ACOL = 2048
OC = 16
OR = 128
LEVELS = 12
SURF = 4
NBLK = 16
ACOLS = 524288
OCH = 76
NCOL = 1024
NROW = 512
N_LEV = 4
N_TILE = 64


def draw_fold_map(key, part):
    key = jax.random.fold_in(key, 7)
    seam = jax.random.randint(key, (), 0, NCOL)
    columns = jnp.arange(NCOL, dtype=jnp.int32)
    return ((seam - 1 - columns) % NCOL).astype(jnp.int32)


def shared_counts(key):
    count_key = jax.random.fold_in(key, 11)
    counts = jax.random.randint(count_key, (N_TILE, N_LEV), 1, PAIRS + 1)
    counts = counts.at[0, 0].set(PAIRS)
    counts = counts.at[0, 1].set(1)
    return counts.astype(jnp.int32)


def draw_pair_count(key, part):
    counts = shared_counts(key)
    return counts


def draw_margin(key, part):
    counts = shared_counts(key)
    key = jax.random.fold_in(key, 13)
    cell_count = jnp.repeat(jnp.repeat(counts, OC, axis=0), OR, axis=1)
    keys = jax.random.split(key, 5)
    shape_full = (PAIRS, BLK, NCOL, NROW)
    shape_peaks = (8, NCOL, NROW)
    background = jnp.exp(jax.random.uniform(keys[1], shape_full, jnp.float32, math.log(0.0005), math.log(0.002)))
    peaks = jnp.exp(jax.random.uniform(keys[2], shape_peaks, jnp.float32, math.log(0.1), 0.0))
    active = jax.random.randint(keys[0], (NCOL, NROW), 2, 9)
    slots = jax.random.randint(keys[3], shape_peaks, 0, 840) % cell_count[None]
    columns = jax.random.randint(keys[4], shape_peaks, 0, BLK)
    slot_ids = jnp.arange(PAIRS, dtype=jnp.int32)[:, None, None, None]
    column_ids = jnp.arange(BLK, dtype=jnp.int32)[None, :, None, None]
    weights = background
    for index in range(8):
        live = (index < active)[None, None]
        hit = (slot_ids == slots[index][None, None]) & (column_ids == columns[index][None, None]) & live
        weights = jnp.where(hit, peaks[index][None, None], weights)
    return weights.astype(jnp.bfloat16)


def set_ends(values, rng, least, largest):
    longest = values.shape.index(max(values.shape))
    spots = []
    for shift in (0, 1):
        where = [jax.random.randint(jax.random.fold_in(rng, axis), (), 0, length) for axis, length in enumerate(values.shape)]
        where[longest] = (where[longest] + shift) % values.shape[longest]
        spots.append(tuple(where))
    return values.at[spots[0]].set(least).at[spots[1]].set(largest)


def shard_levels(key, extent, shards, least, largest):
    factor_of = 1.0
    for position, blocks in shards:
        draws = jax.random.uniform(jax.random.fold_in(jax.random.fold_in(key, 6), position), (blocks,), jnp.float32, least / len(shards), largest / len(shards))
        factor_of = factor_of * jnp.repeat(jnp.exp(draws), extent[position] // blocks).reshape((-1,) + (1,) * (len(extent) - 1 - position))
    return factor_of


def bell_draw(stream_key, shape, spread, bound, cuts=(), kind=jnp.bfloat16):
    array = spread * jax.random.normal(stream_key, shape, jnp.float32)
    if cuts:
        array = array * shard_levels(stream_key, shape, cuts, -0.22, 0.18)
    return jnp.clip(array, -bound, bound).astype(kind)


def setup_inputs(seed: int = 0) -> dict:
    arg_keys = jax.random.split(jax.random.key(seed), 17)
    atm_state = bell_draw(arg_keys[0], (LEVELS, FIELDS, ACOLS), 1.0, 6.0, ((0, 4), (2, 64)))
    surface = bell_draw(arg_keys[1], (SURF, ACOLS), 1.0, 6.0, ((0, 4), (1, 64)))
    mlp_in = bell_draw(arg_keys[2], (LEVELS * FIELDS + SURF, HID), (LEVELS * FIELDS + SURF) ** -0.5, 0.625)
    mlp_mid = bell_draw(arg_keys[3], (HID, HID), HID ** -0.5, 0.25)
    mlp_out = bell_draw(arg_keys[4], (HID, LEVELS * FIELDS), HID ** -0.5, 0.25)
    mlp_flux = bell_draw(arg_keys[5], (HID, FLUX), HID ** -0.5, 0.25)
    ocean_state = bell_draw(arg_keys[6], (OCH, NCOL, NROW), 1.0, 6.0, ((1, 64), (2, 4)))
    ocean_mask = set_ends((jax.random.randint(arg_keys[7], (NCOL, NROW), 0, 10) < 7).astype(jnp.int32), jax.random.fold_in(arg_keys[7], 1), 0, 1)
    fold_map = draw_fold_map(jax.random.fold_in(arg_keys[16], 71), 0)
    pair_tile = set_ends(jax.random.randint(arg_keys[9], (N_TILE, N_LEV, PAIRS), 0, N_TILE), jax.random.fold_in(arg_keys[9], 1), 0, N_TILE - 1).astype(jnp.int32)
    pair_block = set_ends(jax.random.randint(arg_keys[10], (N_TILE, N_LEV, PAIRS), 0, NBLK), jax.random.fold_in(arg_keys[10], 1), 0, NBLK - 1).astype(jnp.int32)
    pair_count = draw_pair_count(jax.random.fold_in(arg_keys[16], 71), 0)
    margin = draw_margin(jax.random.fold_in(arg_keys[16], 71), 0)
    conv_in = bell_draw(arg_keys[13], (3, 3, OCH + FLUX, CH), (9 * (OCH + FLUX)) ** -0.5, 0.21875)
    conv_mid = bell_draw(arg_keys[14], (3, 3, CH, CH), (9 * CH) ** -0.5, 0.125)
    conv_out = bell_draw(arg_keys[15], (3, 3, CH, OCH), (9 * CH) ** -0.5, 0.125)
    return dict(atm_state=atm_state, surface=surface, mlp_in=mlp_in, mlp_mid=mlp_mid, mlp_out=mlp_out, mlp_flux=mlp_flux, ocean_state=ocean_state, ocean_mask=ocean_mask, fold_map=fold_map, pair_tile=pair_tile, pair_block=pair_block, pair_count=pair_count, margin=margin, conv_in=conv_in, conv_mid=conv_mid, conv_out=conv_out)


def column_block(inputs, mlp_in, mlp_mid, mlp_out, mlp_flux):
    level_rows, surface_rows = inputs
    stacked = jnp.concatenate([level_rows, surface_rows], axis=0)
    first = jax.nn.gelu(jnp.dot(mlp_in.T, stacked, preferred_element_type=jnp.float32)).astype(jnp.bfloat16)
    second = jax.nn.gelu(jnp.dot(mlp_mid.T, first, preferred_element_type=jnp.float32)).astype(jnp.bfloat16)
    change = jnp.dot(mlp_out.T, second, preferred_element_type=jnp.float32)
    updated = (level_rows.astype(jnp.float32) + change).astype(jnp.bfloat16)
    fluxes = jnp.dot(mlp_flux.T, second, preferred_element_type=jnp.float32).astype(jnp.bfloat16)
    return updated, fluxes


def pad_grid(grid, fold_map):
    wrapped = jnp.concatenate([grid[:, -1:], grid, grid[:, :1]], axis=1)
    folded = grid[:, fold_map, -1]
    folded = jnp.concatenate([folded[:, -1:], folded, folded[:, :1]], axis=1)
    lower = jnp.zeros_like(wrapped[:, :, :1])
    return jnp.concatenate([lower, wrapped, folded[:, :, None]], axis=2)


def convolve(piece, kernel):
    span_x = piece.shape[1] - 2
    span_y = piece.shape[2] - 2
    result = jnp.zeros((kernel.shape[3], span_x, span_y), jnp.float32)
    for shift_x in range(3):
        for shift_y in range(3):
            window = piece[:, shift_x:shift_x + span_x, shift_y:shift_y + span_y]
            result = result + jnp.einsum("co,cxy->oxy", kernel[shift_x, shift_y].astype(jnp.float32), window.astype(jnp.float32))
    return result


def convolve_all(extended, kernel):
    def band(band_id):
        piece = lax.dynamic_slice_in_dim(extended, band_id * OC, OC + 2, 1)
        return convolve(piece, kernel)
    pieces = lax.map(band, jnp.arange(N_TILE, dtype=jnp.int32))
    return pieces.transpose(1, 0, 2, 3).reshape(kernel.shape[3], NCOL, NROW)


def reference(atm_state, surface, mlp_in, mlp_mid, mlp_out, mlp_flux, ocean_state, ocean_mask, fold_map, pair_tile, pair_block, pair_count, margin, conv_in, conv_mid, conv_out):
    rows_atm = LEVELS * FIELDS
    blocks_all = ACOLS // ACOL
    level_flat = atm_state.reshape(rows_atm, blocks_all, ACOL).transpose(1, 0, 2)
    surface_flat = surface.reshape(SURF, blocks_all, ACOL).transpose(1, 0, 2)

    def run_block(inputs):
        return column_block(inputs, mlp_in, mlp_mid, mlp_out, mlp_flux)

    updated, fluxes = lax.map(run_block, (level_flat, surface_flat))
    atm_next = updated.transpose(1, 0, 2).reshape(LEVELS, FIELDS, ACOLS)
    flux_all = fluxes.transpose(1, 0, 2).reshape(FLUX, ACOLS)

    lev_ids = jnp.arange(N_LEV, dtype=jnp.int32)
    starts = pair_tile * (N_LEV * ACOL) + lev_ids[None, :, None] * ACOL + pair_block * BLK
    offsets = (starts[..., None] + jnp.arange(BLK, dtype=jnp.int32)).astype(jnp.int32)
    picked = flux_all[:, offsets]
    used = (jnp.arange(PAIRS, dtype=jnp.int32)[None, None, :] < pair_count[:, :, None]).astype(jnp.float32)
    weights_tiles = margin.reshape(PAIRS, BLK, N_TILE, OC, N_LEV, OR).transpose(2, 0, 1, 3, 4, 5)

    def regrid_tile(inputs):
        picked_tile, used_tile, weight_tile = inputs
        weight_float = weight_tile.astype(jnp.float32)
        numer = jnp.einsum("flpb,lp,pbxlr->fxlr", picked_tile.astype(jnp.float32), used_tile, weight_float)
        denom = jnp.einsum("lp,pbxlr->xlr", used_tile, weight_float)
        return (numer / denom[None]).astype(jnp.bfloat16).reshape(FLUX, OC, NROW)

    regridded = lax.map(regrid_tile, (picked.transpose(1, 0, 2, 3, 4), used, weights_tiles))
    ocean_flux = regridded.transpose(1, 0, 2, 3).reshape(FLUX, NCOL, NROW)

    land_sea = ocean_mask.astype(jnp.float32)
    combined = jnp.concatenate([ocean_state, ocean_flux], axis=0)
    hidden_one = (jax.nn.gelu(convolve_all(pad_grid(combined, fold_map), conv_in)) * land_sea).astype(jnp.bfloat16)
    hidden_two = (jax.nn.gelu(convolve_all(pad_grid(hidden_one, fold_map), conv_mid)) * land_sea).astype(jnp.bfloat16)
    change = convolve_all(pad_grid(hidden_two, fold_map), conv_out)
    ocean_next = ((ocean_state.astype(jnp.float32) + change) * land_sea).astype(jnp.bfloat16)
    return atm_next, ocean_next
```

```python
import jax
import jax.numpy as jnp
from jax import lax
from jax.experimental import pallas as pl
from jax.experimental.pallas import tpu as pltpu
from jax.sharding import PartitionSpec as P

BF = jnp.bfloat16
F32 = jnp.float32
I32 = jnp.int32
SLAB = 8
HALO = 3
PITCH = 144
LANES = 128
VMEM = 56 * 1024 * 1024
C1 = 0.7978845608028654
C2 = C1 * 0.044715


def gelu(x):
    half = 0.5 * x
    return half * jnp.tanh(x * (C1 + C2 * (x * x))) + half


def dot(a, b):
    return jnp.dot(a, b, preferred_element_type=F32)


def dot_nt(a, b):
    return lax.dot_general(a, b, (((1,), (1,)), ((), ())), preferred_element_type=F32)


def iota(shape, dim):
    return lax.broadcasted_iota(I32, shape, dim)


def vmem_specs(n):
    return [pl.BlockSpec(memory_space=pltpu.VMEM)] * n


def smem_spec():
    return pl.BlockSpec(memory_space=pltpu.SMEM)


def params():
    return pltpu.CompilerParams(vmem_limit_bytes=VMEM)


def mlp_kernel(code_ref, z_ref, w1_ref, w2_ref, w3_ref, up_ref, send_ref, blocks, sends):
    rows, cols = z_ref.shape
    step = 512
    for c in range(0, cols, step):
        z = z_ref[:, c : c + step]
        first = gelu(dot(w1_ref[...], z)).astype(BF)
        second = gelu(dot(w2_ref[...], first)).astype(BF)
        out = dot(w3_ref[...], second)
        up_ref[:, c : c + step] = (z.astype(F32) + out[:rows]).astype(BF)
        for k in range(step // 128):
            blocks[c // 128 + k] = out[rows : rows + 8, 128 * k : 128 * k + 128].astype(BF).astype(F32)
    for i in range(send_ref.shape[0] * 4):
        code = code_ref[i]
        block = blocks[jnp.maximum(code, 0)]
        sends[i // 4, 8 * (i % 4) : 8 * (i % 4) + 8] = jnp.where(code >= 0, block, 0.0)
    send_ref[...] = sends[...].astype(BF)


def column_model(code, z, w1, w2, w3, tiles):
    rows, cols = z.shape
    return pl.pallas_call(
        mlp_kernel,
        in_specs=[smem_spec()] + vmem_specs(4),
        out_specs=vmem_specs(2),
        out_shape=[
            jax.ShapeDtypeStruct((rows, cols), BF),
            jax.ShapeDtypeStruct((tiles, 32, 128), BF),
        ],
        scratch_shapes=[pltpu.VMEM((cols // 128, 8, 128), F32), pltpu.VMEM((tiles, 32, 128), F32)],
        compiler_params=params(),
        cost_estimate=pl.CostEstimate(flops=3 * 10**9, bytes_accessed=2 * 10**6, transcendentals=0),
        name="column_model",
    )(code, z, w1, w2, w3)


def remap_kernel(scal_ref, got_ref, margin_ref, flux_ref, send_ref):
    tiles = got_ref.shape[0]
    count, tile = scal_ref[4], scal_ref[5]
    pieces = []
    for p in range(4):
        piece = got_ref[scal_ref[p]].astype(F32)[8 * p : 8 * p + 8]
        pieces.append(jnp.where(p < count, piece, 0.0))
    blocks = jnp.concatenate(pieces, axis=0).astype(BF)
    spread = (iota((128, 2048), 0) == iota((128, 2048), 1) // 16).astype(BF)
    wide = dot(blocks, spread)
    same = iota((16, 2048), 0) == iota((16, 2048), 1) % 16
    total = None
    for p in range(4):
        rows = jnp.broadcast_to(wide[8 * p : 8 * p + 8][None], (16, 8, 2048))
        rows = jnp.where(same[:, None, :], rows, 0.0).reshape(128, 2048)
        ones = jnp.where(same & (p < count), 1.0, 0.0)
        left = jnp.concatenate([rows, ones], axis=0).astype(BF)
        term = dot(left, margin_ref[2048 * p : 2048 * p + 2048])
        total = term if total is None else total + term
    numer = total[:128].reshape(16, 8, 128)
    flux = (numer / total[128:144][:, None, :]).reshape(128, 128).astype(BF)
    flux_ref[...] = flux
    wide = flux.astype(F32)
    top = dot_nt((iota((8, 128), 1) == 127 - iota((8, 128), 0)).astype(BF), flux)
    plain = jnp.concatenate([top, jnp.zeros((24, 128), F32)], axis=0).astype(BF)
    send_ref[...] = jnp.broadcast_to(plain[None], (tiles, 32, 128))
    send_ref[lax.rem(tile + 1, tiles)] = jnp.concatenate([top, wide[104:128]], axis=0).astype(BF)
    send_ref[lax.rem(tile + tiles - 1, tiles)] = jnp.concatenate([top, wide[0:24]], axis=0).astype(BF)


def remap(scal, got, margin):
    return pl.pallas_call(
        remap_kernel,
        in_specs=[smem_spec()] + vmem_specs(2),
        out_specs=vmem_specs(2),
        out_shape=[jax.ShapeDtypeStruct((128, 128), BF), jax.ShapeDtypeStruct(got.shape, BF)],
        compiler_params=params(),
        cost_estimate=pl.CostEstimate(flops=10**9, bytes_accessed=3 * 10**6, transcendentals=0),
        name="remap",
    )(scal, got, margin)


def rim_kernel(scal_ref, got_ref, flux_ref, wide_ref, up_ref, down_ref, fold_ref):
    tiles = got_ref.shape[0]
    tile, seam, shift = scal_ref[5], scal_ref[6], scal_ref[7]
    low = got_ref[lax.rem(tile + tiles - 1, tiles)].astype(F32)[8:32]
    high = got_ref[lax.rem(tile + 1, tiles)].astype(F32)[8:32]
    wide = jnp.concatenate([low, flux_ref[...].astype(F32), high, jnp.zeros((80, 128), F32)], axis=0).astype(BF)
    wide_ref[...] = wide
    row, col = iota((16, 128), 0), iota((16, 128), 1)
    up_ref[...] = dot_nt(((col == 125 + row) & (row < 3)).astype(BF), wide).astype(BF)
    down_ref[...] = dot_nt(((col == row) & (row < 3)).astype(BF), wide).astype(BF)
    total = None
    u, f = iota((128, 256), 0) // 8, iota((128, 256), 0) % 8
    i, g = iota((128, 256), 1) // 8, iota((128, 256), 1) % 8
    for e in (-1, 0, 1, 2):
        strip = got_ref[lax.rem(seam - tile - e + 3 * tiles, tiles)]
        pick = ((f == g) & (u == 16 * e + shift + HALO - i)).astype(BF)
        term = dot(strip, pick)
        total = term if total is None else total + term
    fold_ref[...] = total[:16].astype(BF)


def rim(scal, got, flux):
    strip = jax.ShapeDtypeStruct((16, 256), BF)
    return pl.pallas_call(
        rim_kernel,
        in_specs=[smem_spec()] + vmem_specs(2),
        out_specs=vmem_specs(4),
        out_shape=[jax.ShapeDtypeStruct((256, 128), BF), strip, strip, strip],
        compiler_params=params(),
        cost_estimate=pl.CostEstimate(flops=10**8, bytes_accessed=10**6, transcendentals=0),
        name="rim",
    )(scal, got, flux)


def conv_kernel(
    scal_ref, ext_ref, wide_ref, south_ref, north_ref, fold_ref, w1_ref, w1r_ref, w2_ref, w3_ref, out_ref,
    v3, h3, h2, result,
):
    top = scal_ref[8] == 1
    n0, n1, n2, n3 = 22, 20, 18, 16

    north = jnp.where(top, fold_ref[...].astype(F32), north_ref[...].astype(F32))
    rims = jnp.concatenate([south_ref[...].astype(F32), north], axis=0).astype(BF)
    row, col = iota((PITCH, 128), 0), iota((PITCH, 128), 1)
    fluxes = dot_nt((row == col + 3).astype(BF), wide_ref[...])
    row, col = iota((PITCH, 32), 0), iota((PITCH, 32), 1)
    put = ((col < 3) & (row == col)) | ((col >= 16) & (col < 19) & (row == col - 16 + 131))
    fluxes = fluxes + dot(put.astype(BF), rims)
    lane = iota((PITCH, LANES), 1)

    for x in range(n0):
        start = 8 * x
        part = fluxes[:, 128 * (start // 128) : 128 * (start // 128) + 128]
        part = pltpu.roll(part, (76 - start) % 128, 1)
        v = jnp.where(lane < 76, ext_ref[x].astype(F32), jnp.where(lane < 84, part, 0.0))
        before = pltpu.roll(v, 1, 0)
        here = pltpu.roll(v, 84, 1)
        after = pltpu.roll(pltpu.roll(v, PITCH - 1, 0), 40, 1)
        v3[x, :, 0:128] = jnp.where(lane < 84, before, here).astype(BF)
        v3[x, :, 128:256] = jnp.where(lane < 40, here, after).astype(BF)

    def mask_of(x, lo, size):
        return ext_ref[x, lo : lo + size].astype(F32)[:, 84:85]

    chunk = 5
    for c0 in range(0, n1, chunk):
        acc = None
        for a in range(3):
            d = dot(v3[c0 + a : c0 + a + chunk].reshape(chunk * PITCH, 256), w1_ref[a])
            acc = d if acc is None else acc + d
        acc = acc.reshape(chunk, PITCH, 256)
        for k in range(chunk):
            x = c0 + k
            g = gelu(acc[k]) * mask_of(x + 1, 0, PITCH)
            h3[x, :, 0:256] = pltpu.roll(g, 1, 0).astype(BF)
            h3[x, :, 256:512] = g.astype(BF)
            h3[x, :, 512:768] = pltpu.roll(g, PITCH - 1, 0).astype(BF)

    @pl.when(top)
    def _():
        acc = None
        for a in range(3):
            d = dot(v3[a : a + n1, 128:144, :].reshape(n1 * 16, 256), w1r_ref[a])
            acc = d if acc is None else acc + d
        acc = acc.reshape(n1, 16, 256)
        row = iota((16, 256), 0)
        for x in range(n1):
            g = gelu(acc[x]) * mask_of(x + 1, 128, 16)
            old = h3[x, 128:144, 256:512].astype(F32)
            new = jnp.where((row == 3) | (row == 4), g, old)
            h3[x, 128:144, 256:512] = new.astype(BF)
            old = h3[x, 128:144, 0:256].astype(F32)
            h3[x, 128:144, 0:256] = jnp.where((row == 4) | (row == 5), pltpu.roll(new, 1, 0), old).astype(BF)
            old = h3[x, 128:144, 512:768].astype(F32)
            h3[x, 128:144, 512:768] = jnp.where((row == 2) | (row == 3), pltpu.roll(new, 15, 0), old).astype(BF)

    chunk = 6
    for c0 in range(0, n2, chunk):
        acc = None
        for a in range(3):
            d = dot(h3[c0 + a : c0 + a + chunk].reshape(chunk * PITCH, 768), w2_ref[a])
            acc = d if acc is None else acc + d
        acc = acc.reshape(chunk, PITCH, 256)
        for k in range(chunk):
            x = c0 + k
            h2[x] = (gelu(acc[k]) * mask_of(x + 2, 0, PITCH)).astype(BF)

    @pl.when(top)
    def _():
        acc = None
        for a in range(3):
            for b in range(3):
                lhs = h3[a : a + n2, 128:144, 256 * b : 256 * b + 256].reshape(n2 * 16, 256)
                d = dot(lhs, w2_ref[2 - a, 256 * (2 - b) : 256 * (2 - b) + 256, :])
                acc = d if acc is None else acc + d
        acc = acc.reshape(n2, 16, 256)
        row = iota((16, 256), 0)
        for x in range(n2):
            g = gelu(acc[x]) * mask_of(x + 2, 128, 16)
            old = h2[x, 128:144].astype(F32)
            h2[x, 128:144] = jnp.where(row == 3, g, old).astype(BF)

    chunk = 4
    for c0 in range(0, n3, chunk):
        acc = None
        for a in range(3):
            d = dot(h2[c0 + a : c0 + a + chunk].reshape(chunk * PITCH, 256), w3_ref[a])
            acc = d if acc is None else acc + d
        acc = acc.reshape(chunk, PITCH, 384)
        for k in range(chunk):
            x = c0 + k
            change = (
                pltpu.roll(acc[k][:, 0:128], PITCH - 2, 0)
                + pltpu.roll(acc[k][:, 128:256], PITCH - 3, 0)
                + pltpu.roll(acc[k][:, 256:384], PITCH - 4, 0)
            )
            state = pltpu.roll(ext_ref[x + 3].astype(F32), PITCH - 3, 0)
            new = ((state + change) * state[:, 84:85])[:128]
            result[:, x, :] = new.T[:80]
    out_ref[...] = result[...][:76].astype(BF)


def convolutions(*args):
    return pl.pallas_call(
        conv_kernel,
        in_specs=[smem_spec()] + vmem_specs(len(args) - 1),
        out_specs=vmem_specs(1)[0],
        out_shape=jax.ShapeDtypeStruct((76, 16, 128), BF),
        scratch_shapes=[
            pltpu.VMEM((22, PITCH, 256), BF),
            pltpu.VMEM((20, PITCH, 768), BF),
            pltpu.VMEM((18, PITCH, 256), BF),
            pltpu.VMEM((80, 16, 128), F32),
        ],
        compiler_params=params(),
        cost_estimate=pl.CostEstimate(flops=8 * 10**9, bytes_accessed=8 * 10**6, transcendentals=0),
        name="convolutions",
    )(*args)


def shifted(forth, back, axis, periodic):
    count = lax.axis_size(axis)
    forward = [(i, i + 1) for i in range(count - 1)]
    if periodic:
        forward.append((count - 1, 0))
    backward = [(b, a) for a, b in forward]
    return lax.ppermute(forth, axis, forward), lax.ppermute(back, axis, backward)


def per_tile(x):
    return lax.all_to_all(x, "tile", split_axis=0, concat_axis=0, tiled=True)


def per_device(
    atm_state,
    surface,
    mlp_in,
    mlp_mid,
    mlp_out,
    mlp_flux,
    ocean_state,
    ocean_mask,
    fold_map,
    pair_tile,
    pair_block,
    pair_count,
    margin,
    conv_in,
    conv_mid,
    conv_out,
):
    lev_dev, fields_n, tile_cols = atm_state.shape
    groups = lax.axis_size("lev")
    tiles = lax.axis_size("tile")
    tile = lax.axis_index("tile")
    at_top = lax.axis_index("lev") == groups - 1
    per_col = tile_cols // groups
    rows_dev = lev_dev * SLAB
    hid = mlp_mid.shape[0]
    och, span_x, span_y = ocean_state.shape
    pairs, blk = margin.shape[0], margin.shape[1]
    s = fold_map[0] + 1
    seam, shift = (s - 1) // span_x, (s - 1) % span_x

    extra = jnp.pad(surface[None], ((0, lev_dev - 1), (0, SLAB - fields_n - 1), (0, 0)))
    packed = jnp.concatenate([atm_state, extra], axis=1).reshape(rows_dev, groups, per_col)
    z = lax.all_to_all(packed, "lev", split_axis=1, concat_axis=0, tiled=True).reshape(groups * rows_dev, per_col)

    state = jnp.concatenate(
        [
            ocean_state,
            jnp.zeros((8, span_x, span_y), BF),
            ocean_mask.astype(BF)[None],
            jnp.zeros((LANES - och - 9, span_x, span_y), BF),
        ],
        axis=0,
    ).transpose(1, 2, 0)
    ask = jnp.concatenate([pair_tile[0, 0], pair_block[0, 0], jnp.broadcast_to(pair_count[0], (4,))])
    ask = jnp.pad(ask.astype(BF), (0, LANES - 12))[None]
    strip = jnp.concatenate(
        [state[:, span_y - 3 :].reshape(3 * span_x, LANES), ask, jnp.zeros((15, LANES), BF)], axis=0
    )
    strips = per_tile(jnp.broadcast_to(strip[None], (tiles,) + strip.shape))
    asked = strips[:, 3 * span_x, :12].astype(I32)
    slot = jnp.arange(pairs, dtype=I32)[None, :]
    mine = (asked[:, 0:4] == tile) & (slot < asked[:, 8:12])
    code = jnp.where(mine, asked[:, 4:8], -1).reshape(tiles * pairs)

    def to_rows(w, extra):
        w = w.reshape(groups, lev_dev, fields_n, hid)
        extra = jnp.pad(extra.reshape(groups, 1, 1, hid), ((0, 0), (0, lev_dev - 1), (0, 0), (0, 0)))
        pad = jnp.zeros((groups, lev_dev, SLAB - fields_n - 1, hid), BF)
        return jnp.concatenate([w, extra, pad], axis=2).reshape(groups * rows_dev, hid)

    rows_atm = groups * lev_dev * fields_n
    w1 = to_rows(mlp_in[:rows_atm], mlp_in[rows_atm:]).T
    w3 = jnp.concatenate([to_rows(mlp_out.T, jnp.zeros((groups, hid), BF)), mlp_flux.T], axis=0)

    updated, send = column_model(code, z, w1, mlp_mid.T, w3, tiles)
    got = per_tile(send)

    back = lax.all_to_all(updated.reshape(groups, rows_dev, per_col), "lev", split_axis=0, concat_axis=0, tiled=True)
    atm_next = back.transpose(1, 0, 2).reshape(lev_dev, SLAB, tile_cols)[:, :fields_n]

    x_, k_ = jnp.arange(3 * span_x)[:, None] // 3, jnp.arange(3 * span_x)[:, None] % 3
    e_ = jnp.arange(6 * span_x)[None, :] // (3 * span_x)
    u_, r_ = (jnp.arange(6 * span_x)[None, :] // 3) % span_x, jnp.arange(6 * span_x)[None, :] % 3
    pick = ((u_ == span_x * e_ + shift - x_) & (r_ == 2 - k_)).astype(BF)
    both = jnp.concatenate(
        [
            lax.dynamic_index_in_dim(strips, jnp.mod(seam - tile - e, tiles), 0, keepdims=False)[: 3 * span_x]
            for e in range(2)
        ],
        axis=0,
    )
    folded = dot(pick, both).astype(BF).reshape(span_x, 3, LANES)
    south, north = shifted(state[:, span_y - 3 :], state[:, :3], "lev", False)
    north = jnp.where(at_top, folded, north)
    pad = jnp.zeros((span_x, PITCH - span_y - 6, LANES), BF)
    tall = jnp.concatenate([south, state, north, pad], axis=1)
    west, east = shifted(tall[span_x - 3 :], tall[:3], "tile", True)
    ext = jnp.concatenate([west, tall, east], axis=0)

    cw1 = jnp.pad(conv_in.reshape(3, 3 * (och + 8), -1), ((0, 0), (0, 256 - 3 * (och + 8)), (0, 0)))
    cw1r = conv_in[::-1, ::-1].reshape(3, 3 * (och + 8), -1)
    cw1r = jnp.pad(cw1r, ((0, 0), (0, 256 - 3 * (och + 8)), (0, 0)))
    ch = conv_mid.shape[2]
    cw2 = conv_mid.reshape(3, 3 * ch, ch)
    cw3 = jnp.pad(conv_out, ((0, 0), (0, 0), (0, 0), (0, 128 - och))).transpose(0, 2, 1, 3).reshape(3, ch, 384)

    scal = jnp.stack(
        [pair_tile[0, 0, p] for p in range(4)] + [pair_count[0, 0], tile, seam, shift, at_top.astype(I32)]
    ).astype(I32)
    flux, send = remap(scal, got, margin.reshape(pairs * blk * span_x, span_y))
    wide, up, down, fold = rim(scal, per_tile(send), flux)
    south, north = shifted(up, down, "lev", False)
    ocean_next = convolutions(scal, ext, wide, south, north, fold, cw1, cw1r, cw2, cw3)
    return (atm_next, ocean_next)


def solution(mesh):
    return jax.shard_map(
        per_device,
        mesh=mesh,
        in_specs=(
            P("lev", None, "tile"),
            P("lev", "tile"),
            P(),
            P(),
            P(),
            P(),
            P(None, "tile", "lev"),
            P("tile", "lev"),
            P(),
            P("tile", "lev", None),
            P("tile", "lev", None),
            P("tile", "lev"),
            P(None, None, "tile", "lev"),
            P(),
            P(),
            P(),
        ),
        out_specs=(P("lev", None, "tile"), P(None, "tile", "lev")),
        check_vma=False,
    )
```

```python
import jax
import jax.numpy as jnp
from jax import lax
from jax.experimental import pallas as pl
from jax.experimental.pallas import tpu as pltpu
from jax.sharding import PartitionSpec as P

BF = jnp.bfloat16
F32 = jnp.float32
I32 = jnp.int32
SLAB = 8
HALO = 3
ZS, CS = 8, 2
PITCH = 144
LANES = 128
MIB = 1024 * 1024
C1 = 0.7978845608028654
C2 = C1 * 0.044715


def gelu(x):
    half = 0.5 * x
    return half * jnp.tanh(x * (C1 + C2 * (x * x))) + half


def dot(a, b):
    return jnp.dot(a, b, preferred_element_type=F32)


def dot_nt(a, b):
    return lax.dot_general(a, b, (((1,), (1,)), ((), ())), preferred_element_type=F32)


def iota(shape, dim):
    return lax.broadcasted_iota(I32, shape, dim)


def vmem_specs(n):
    return [pl.BlockSpec(memory_space=pltpu.VMEM)] * n


def hbm_specs(n):
    return [pl.BlockSpec(memory_space=pltpu.HBM)] * n


def in_hbm(*arrays):
    return [pltpu.with_memory_space_constraint(x, pltpu.HBM) for x in arrays]


def fetch(pairs, sems):
    copies = [pltpu.make_async_copy(a, b, sems.at[i]) for i, (a, b) in enumerate(pairs)]
    for copy in copies:
        copy.start()
    return copies


def smem_spec():
    return pl.BlockSpec(memory_space=pltpu.SMEM)


def params(mib):
    return pltpu.CompilerParams(vmem_limit_bytes=mib * MIB)


def place():
    tile = lax.axis_index("tile")
    return tile, lax.rem(tile // CS, ZS)


def collect_kernel(atm_ref, surface_ref, *refs):
    *out_refs, atm, surface, sems = refs
    levels, _, cols = atm_ref.shape
    parts = len(out_refs)
    size = cols // parts
    lev = lax.axis_index("lev")
    zero = jnp.zeros((1, size), F32)
    spans = [pl.ds(pl.multiple_of(lax.rem(lev + k, parts) * size, size), size) for k in range(parts)]
    order = (1, 2, 3, 0)
    copies = fetch([(surface_ref, surface)] + [(atm_ref.at[:, :, spans[k]], atm.at[k]) for k in order], sems)
    copies[0].wait()
    for i, k in enumerate(order):
        copies[1 + i].wait()
        rows = []
        for j in range(levels):
            extra = surface[:, spans[k]].astype(F32) if j == 0 else zero
            rows += [atm[k, j].astype(F32), extra, zero]
        out_refs[k][...] = jnp.concatenate(rows, axis=0).astype(BF)


def collect(atm, surface, parts):
    levels, _, cols = atm.shape
    return pl.pallas_call(
        collect_kernel,
        in_specs=hbm_specs(2),
        out_specs=vmem_specs(parts),
        out_shape=[jax.ShapeDtypeStruct((levels * SLAB, cols // parts), BF)] * parts,
        scratch_shapes=[
            pltpu.VMEM((parts, levels, 6, cols // parts), BF),
            pltpu.VMEM((1, cols), BF),
            pltpu.SemaphoreType.DMA((parts + 1,)),
        ],
        compiler_params=params(8),
        cost_estimate=pl.CostEstimate(flops=10**6, bytes_accessed=10**6, transcendentals=0),
        name="collect",
    )(*in_hbm(atm, surface))


def spread_kernel(*refs):
    back_refs, out_ref = refs[:-1], refs[-1]
    parts, size = len(back_refs), back_refs[0].shape[1]
    lev = lax.axis_index("lev")
    for k in range(parts):
        rows = back_refs[k][...].astype(F32)
        span = pl.ds(pl.multiple_of(lax.rem(lev + k, parts) * size, size), size)
        for j in range(out_ref.shape[0]):
            out_ref[j, :, span] = rows[SLAB * j : SLAB * j + 6].astype(BF)


def spread(back, levels):
    parts, size = len(back), back[0].shape[1]
    return pl.pallas_call(
        spread_kernel,
        in_specs=vmem_specs(parts),
        out_specs=vmem_specs(1)[0],
        out_shape=jax.ShapeDtypeStruct((levels, 6, parts * size), BF),
        compiler_params=params(8),
        cost_estimate=pl.CostEstimate(flops=10**6, bytes_accessed=10**6, transcendentals=0),
        name="spread",
    )(*back)


def asking_kernel(count_ref, tile_in, block_in, fold_in, out_ref, seam_ref, tile_ref, block_ref, fold_ref, sems):
    pairs = [(tile_in, tile_ref), (block_in, block_ref), (fold_in, fold_ref)]
    for copy in fetch(pairs, sems):
        copy.wait()
    seam_ref[0] = fold_ref[0]
    for p in range(4):
        seam_ref[1 + p] = tile_ref[0, 0, p]
    seam_ref[5] = count_ref[0, 0]
    rows, zs = [], []
    for p in range(4):
        source, block = tile_ref[0, 0, p], block_ref[0, 0, p]
        number = (source // (CS * ZS) * CS + lax.rem(source, CS)) * 16 + block
        z = jnp.where(p < count_ref[0, 0], lax.rem(source // CS, ZS), -1)
        rows.append(jnp.full((1, 128), number, I32))
        zs.append(jnp.full((1, 128), z, I32))
    out_ref[0] = jnp.concatenate(rows + zs + [jnp.zeros((8, 128), I32)], axis=0).astype(F32).astype(BF)


def asking(tile, block, count, fold_map):
    return pl.pallas_call(
        asking_kernel,
        in_specs=[smem_spec()] + hbm_specs(3),
        out_specs=vmem_specs(1) + [smem_spec()],
        out_shape=[jax.ShapeDtypeStruct((1, 16, 128), BF), jax.ShapeDtypeStruct((8,), I32)],
        scratch_shapes=[pltpu.SMEM(x.shape, I32) for x in (tile, block, fold_map)]
        + [pltpu.SemaphoreType.DMA((3,))],
        compiler_params=params(4),
        cost_estimate=pl.CostEstimate(flops=10**6, bytes_accessed=10**5, transcendentals=0),
        name="asking",
    )(count, *in_hbm(tile, block, fold_map))


def prepare_kernel(
    state_in, mask_in, win_in, wmid_in, wout_in, wflux_in, state_ref, w1_ref, w2_ref, w3_ref,
    state, mask_ref, win_ref, wmid_ref, wout_ref, wflux_ref, rows, sems,
):
    copies = fetch(
        [
            (state_in, state), (mask_in, mask_ref), (win_in, win_ref), (wmid_in, wmid_ref), (wout_in, wout_ref),
            (wflux_in, wflux_ref),
        ],
        sems,
    )
    channels, cols, size = state_in.shape
    copies[0].wait()
    copies[1].wait()
    rows[...] = state[...].reshape(channels * cols, size).astype(F32)
    for x in range(cols):
        part = rows[pl.ds(x, channels, stride=cols), :]
        mask = mask_ref[x : x + 1].astype(F32)
        part = jnp.concatenate(
            [part, jnp.zeros((84 - channels, size), F32), mask, jnp.zeros((LANES - 85, size), F32)], axis=0
        )
        state_ref[x] = part.T.astype(BF)
    for copy in copies[2:]:
        copy.wait()
    lev = lax.axis_index("lev")
    rows_all = w1_ref.shape[1]
    size = rows_all // 4

    def origin(shape):
        row = iota(shape, 0)
        group = (lev - row // size) & 3
        level, field = 3 * group + row % size // 8, row % 8
        return jnp.where((field < 6) & (row < rows_all), 6 * level + field, -1), group, row

    source, group, row = origin((rows_all, 76))
    source = jnp.where(row % size == 6, 72 + group, source)
    w1_ref[...] = dot((iota((rows_all, 76), 1) == source).astype(BF), win_ref[...]).T.astype(BF)
    source, group, row = origin((rows_all + 8, 72))
    w3 = dot((iota((rows_all + 8, 72), 1) == source).astype(BF), wout_ref[...])
    w3 = w3 + dot((iota((rows_all + 8, 8), 1) == iota((rows_all + 8, 8), 0) - rows_all).astype(BF), wflux_ref[...])
    w3_ref[...] = w3.astype(BF)
    w2_ref[...] = wmid_ref[...].T


def prepare(state, mask, *weights):
    channels, cols, size = state.shape
    hid = weights[1].shape[0]
    return pl.pallas_call(
        prepare_kernel,
        in_specs=hbm_specs(6),
        out_specs=vmem_specs(4),
        out_shape=[
            jax.ShapeDtypeStruct((cols, size, LANES), BF),
            jax.ShapeDtypeStruct((hid, 96), BF),
            jax.ShapeDtypeStruct((hid, hid), BF),
            jax.ShapeDtypeStruct((104, hid), BF),
        ],
        scratch_shapes=[pltpu.VMEM(state.shape, BF), pltpu.VMEM(mask.shape, I32)]
        + [pltpu.VMEM(w.shape, BF) for w in weights]
        + [pltpu.VMEM((channels * cols, size), F32), pltpu.SemaphoreType.DMA((6,))],
        compiler_params=params(12),
        cost_estimate=pl.CostEstimate(flops=10**9, bytes_accessed=10**6, transcendentals=0),
        name="prepare",
    )(*in_hbm(state, mask, *weights))


def mlp_kernel(z0_ref, z1_ref, z2_ref, z3_ref, w1_ref, w2_ref, w3_ref, state_ref, *out_refs):
    z_refs, up_refs, send_ref = (z0_ref, z1_ref, z2_ref, z3_ref), out_refs[:4], out_refs[4]
    size, cols = z0_ref.shape
    rows = 4 * size
    step = 512
    w1, w2, w3 = w1_ref[...], w2_ref[...], w3_ref[...]
    for c in range(0, cols, step):
        z = jnp.concatenate([ref[:, c : c + step].astype(F32) for ref in z_refs], axis=0)
        first = gelu(dot(w1, z.astype(BF))).astype(BF)
        second = gelu(dot(w2, first)).astype(BF)
        out = dot(w3, second)
        for k in range(4):
            span = slice(size * k, size * k + size)
            up = z[span] + out[span]
            if k == 1 or k == 3:
                rim = []
                for x in range(c // 128, (c + step) // 128):
                    tile = state_ref[x, 0:16] if k == 1 else state_ref[x, 112:128]
                    rim.append(tile.astype(F32)[:8] if k == 1 else tile.astype(F32)[8:])
                up = jnp.concatenate([up, jnp.concatenate(rim, axis=1)], axis=0)
            up_refs[k][:, c : c + step] = up.astype(BF)
        for k in range(0, step, 256):
            both = jnp.concatenate([out[rows : rows + 8, k : k + 128], out[rows : rows + 8, k + 128 : k + 256]], axis=0)
            send_ref[0, (c + k) // 256] = both.astype(BF)
    row, col = iota((48, 256), 0), iota((48, 256), 1)
    pick = (col == row // 3 * 16 + 13 + row % 3).astype(BF)
    strip = dot(pick, state_ref[:, 112:128].reshape(256, 128)).astype(BF)
    send_ref[0, 8:11] = strip.reshape(3, 16, 128)
    for j in range(1, send_ref.shape[0]):
        send_ref[j] = send_ref[0]


def column_model(pieces, w1, w2, w3, state):
    size, cols = pieces[0].shape
    return pl.pallas_call(
        mlp_kernel,
        in_specs=vmem_specs(8),
        out_specs=vmem_specs(5),
        out_shape=[
            jax.ShapeDtypeStruct((size, cols), BF),
            jax.ShapeDtypeStruct((size + 8, cols), BF),
            jax.ShapeDtypeStruct((size, cols), BF),
            jax.ShapeDtypeStruct((size + 8, cols), BF),
            jax.ShapeDtypeStruct((8, 11, 16, 128), BF),
        ],
        compiler_params=params(20),
        cost_estimate=pl.CostEstimate(flops=3 * 10**9, bytes_accessed=2 * 10**6, transcendentals=0),
        name="column_model",
    )(*pieces, w1, w2, w3, state)


def pack_kernel(seam_ref, near_ref, far_ref, got_ref, send_ref):
    tile, z_me = place()
    number, zs = [], []
    for m in range(ZS):
        ask = (near_ref if m < 4 else far_ref)[m % 4].astype(F32).astype(I32)
        for p in range(4):
            number.append(jnp.broadcast_to(ask[p : p + 1], (8, 128)))
            zs.append(jnp.broadcast_to(ask[4 + p : 5 + p], (8, 128)))
    number, zs = jnp.concatenate(number, axis=0), jnp.concatenate(zs, axis=0)
    wanted = jnp.where(zs == z_me, number * 8 + iota((256, 128), 0) % 8, -1)
    total = None
    for j in range(8):
        pick = (wanted == iota((256, 128), 1) + 128 * j).astype(BF)
        term = dot(pick, got_ref[j, 0:8].reshape(128, 128))
        total = term if total is None else total + term
    total = total.astype(BF).reshape(ZS, 2, 16, 128)
    for m in range(ZS):
        send_ref[z_me ^ m, 0:2] = total[m]
    key = (seam_ref[0] + HALO) // 16 - 1 + 128
    core = lax.rem(tile, CS)
    z_to = lax.rem(key - lax.rem(key - core, CS) - CS * z_me, CS * ZS) // CS
    source = lax.rem(key - (tile - CS * z_me + CS * z_to), 64)
    strip = got_ref[source // (CS * ZS) * CS + lax.rem(source, CS), 8:11]
    for z in range(ZS):
        send_ref[z, 2:5] = strip


def pack(seam, near, far, got):
    return pl.pallas_call(
        pack_kernel,
        in_specs=[smem_spec()] + vmem_specs(3),
        out_specs=vmem_specs(1)[0],
        out_shape=jax.ShapeDtypeStruct((ZS, 5, 16, 128), BF),
        compiler_params=params(8),
        cost_estimate=pl.CostEstimate(flops=10**8, bytes_accessed=10**6, transcendentals=0),
        name="pack",
    )(seam, near, far, got)


def tall(state_ref, south_ref, north_ref, x):
    size = south_ref.shape[0] - 8
    lanes = slice(LANES * x, LANES * x + LANES)
    south = jnp.where(lax.axis_index("lev") > 0, south_ref[:, lanes].astype(F32)[size:], 0.0)
    return jnp.concatenate([south, state_ref[x].astype(F32), north_ref[:, lanes].astype(F32)[size:]], axis=0)


def remap_kernel(
    seam_ref, got_ref, margin_ref, state_ref, south_ref, north_ref,
    flux_ref, east_ref, west_ref, top_ref, strip_ref,
):
    partner = lax.rem((seam_ref[0] + HALO) // 16 - 1 - lax.axis_index("tile") + 128, 64)
    strip = got_ref[lax.rem(partner // CS, ZS), 2:5]
    strip_ref[...] = strip
    for side_ref, x in ((east_ref, 13), (west_ref, 0)):
        for k in range(HALO):
            side_ref[PITCH * k : PITCH * k + PITCH] = tall(state_ref, south_ref, north_ref, x + k).astype(BF)
        side_ref[432:480] = strip.reshape(48, 128)
    count = seam_ref[5]
    pieces = []
    for p in range(4):
        source = jnp.clip(seam_ref[1 + p], 0, 63)
        piece = got_ref[lax.rem(source // CS, ZS), p // 2].astype(F32)[8 * (p % 2) : 8 * (p % 2) + 8]
        pieces.append(jnp.where(p < count, piece, 0.0))
    blocks = jnp.concatenate(pieces, axis=0).astype(BF)
    spread = (iota((128, 2048), 0) == iota((128, 2048), 1) // 16).astype(BF)
    wide = dot(blocks, spread)
    same = iota((16, 2048), 0) == iota((16, 2048), 1) % 16
    total = None
    for p in range(4):
        rows = jnp.broadcast_to(wide[8 * p : 8 * p + 8][None], (16, 8, 2048))
        rows = jnp.where(same[:, None, :], rows, 0.0).reshape(128, 2048)
        ones = jnp.where(same & (p < count), 1.0, 0.0)
        left = jnp.concatenate([rows, ones], axis=0).astype(BF)
        term = dot(left, margin_ref[2048 * p : 2048 * p + 2048])
        total = term if total is None else total + term
    numer = total[:128].reshape(16, 8, 128)
    flux = (numer / total[128:144][:, None, :]).reshape(128, 128).astype(BF)
    flux_ref[...] = flux
    wide = flux.astype(F32)
    zero = jnp.zeros((8, 128), F32)
    east_ref[480:512] = jnp.concatenate([wide[104:128], zero], axis=0).astype(BF)
    west_ref[480:512] = jnp.concatenate([wide[0:24], zero], axis=0).astype(BF)
    top = dot_nt((iota((8, 128), 1) == 127 - iota((8, 128), 0)).astype(BF), flux).astype(BF)
    top_ref[...] = jnp.broadcast_to(top[None], top_ref.shape)


def remap(seam, got, margin, state, south, north, tiles):
    side = jax.ShapeDtypeStruct((512, 128), BF)
    return pl.pallas_call(
        remap_kernel,
        in_specs=[smem_spec()] + vmem_specs(5),
        out_specs=vmem_specs(5),
        out_shape=[
            jax.ShapeDtypeStruct((128, 128), BF),
            side,
            side,
            jax.ShapeDtypeStruct((tiles, 8, 128), BF),
            jax.ShapeDtypeStruct((3, 16, 128), BF),
        ],
        compiler_params=params(16),
        cost_estimate=pl.CostEstimate(flops=10**9, bytes_accessed=3 * 10**6, transcendentals=0),
        name="remap",
    )(seam, got, margin, state, south, north)


def rim_kernel(low_ref, flux_ref, high_ref, wide_ref, up_ref, down_ref):
    low, high = low_ref[480:512].astype(F32)[:24], high_ref[480:512].astype(F32)[:24]
    wide = jnp.concatenate([low, flux_ref[...].astype(F32), high, jnp.zeros((80, 128), F32)], axis=0).astype(BF)
    wide_ref[...] = wide
    row, col = iota((16, 128), 0), iota((16, 128), 1)
    up_ref[...] = dot_nt(((col == 125 + row) & (row < 3)).astype(BF), wide).astype(BF)
    down_ref[...] = dot_nt(((col == row) & (row < 3)).astype(BF), wide).astype(BF)


def rim(low, flux, high):
    strip = jax.ShapeDtypeStruct((16, 256), BF)
    return pl.pallas_call(
        rim_kernel,
        in_specs=vmem_specs(3),
        out_specs=vmem_specs(3),
        out_shape=[jax.ShapeDtypeStruct((256, 128), BF), strip, strip],
        compiler_params=params(4),
        cost_estimate=pl.CostEstimate(flops=10**8, bytes_accessed=10**6, transcendentals=0),
        name="rim",
    )(low, flux, high)


def conv_kernel(
    seam_ref, state_ref, below_ref, above_ref, west_ref, east_ref, strip_ref, wide_ref, south_ref, north_ref, tops_ref,
    win_in, wmid_in, wout_in, out_ref,
    v3, h3, h2, result, masks, win_ref, w2_ref, wout_ref, w1_ref, w3_ref, sems,
):
    copies = fetch([(win_in, win_ref), (wmid_in, w2_ref), (wout_in, wout_ref)], sems)
    tiles = tops_ref.shape[0]
    tile = lax.axis_index("tile")
    top = lax.axis_index("lev") == lax.axis_size("lev") - 1
    n0, n1, n2, n3 = 22, 20, 18, 16
    seam = (seam_ref[0] + HALO) // 16
    shift = lax.rem(seam_ref[0] + HALO, 16)

    u, f = iota((128, 256), 0) // 8, iota((128, 256), 0) % 8
    i, g = iota((128, 256), 1) // 8, iota((128, 256), 1) % 8
    fold = None
    for e in range(3):
        pick = ((f == g) & (u == 16 * e + shift - i)).astype(BF)
        part = tops_ref[lax.rem(seam - tile - e + 2 * tiles, tiles)].astype(F32)
        term = dot(jnp.concatenate([part, jnp.zeros((8, 128), F32)], axis=0).astype(BF), pick)
        fold = term if fold is None else fold + term
    strips = jnp.concatenate(
        [west_ref[432:480], strip_ref[...].reshape(48, 128), east_ref[432:480]], axis=0
    )
    i, k = iota((352, 144), 0) // 16, iota((352, 144), 0) % 16 - 8
    e, u, r = iota((352, 144), 1) // 48, iota((352, 144), 1) % 48 // 3, iota((352, 144), 1) % 3
    folded = dot(((u == 16 * e + shift - i) & (r == 2 - k) & (k >= 0) & (k < 3)).astype(BF), strips)
    over = iota((16, LANES), 0)
    over = top & (over >= 8) & (over < 11)

    def state_of(x):
        if x < 3:
            v = west_ref[PITCH * x : PITCH * x + PITCH].astype(F32)
        elif x < 19:
            v = tall(state_ref, below_ref, above_ref, x - 3)
        else:
            v = east_ref[PITCH * (x - 19) : PITCH * (x - 19) + PITCH].astype(F32)
        return jnp.concatenate([v[:128], jnp.where(over, folded[16 * x : 16 * x + 16], v[128:])], axis=0)

    north = jnp.where(top, fold, north_ref[...].astype(F32))
    rims = jnp.concatenate([south_ref[...].astype(F32), north], axis=0).astype(BF)
    row, col = iota((PITCH, 128), 0), iota((PITCH, 128), 1)
    fluxes = dot_nt((row == col + 8).astype(BF), wide_ref[...])
    row, col = iota((PITCH, 32), 0), iota((PITCH, 32), 1)
    put = ((col < 3) & (row == col + 5)) | ((col >= 16) & (col < 19) & (row == col - 16 + 136))
    fluxes = fluxes + dot(put.astype(BF), rims)
    lane = iota((PITCH, LANES), 1)

    for x in range(n0):
        start = 8 * x
        part = fluxes[:, 128 * (start // 128) : 128 * (start // 128) + 128]
        part = pltpu.roll(part, (76 - start) % 128, 1)
        state = state_of(x)
        masks[x] = jnp.broadcast_to(state[:, 84:85], (PITCH, 128))
        v = jnp.where(lane < 76, state, jnp.where(lane < 84, part, 0.0))
        before = pltpu.roll(v, 1, 0)
        here = pltpu.roll(v, 84, 1)
        after = pltpu.roll(pltpu.roll(v, PITCH - 1, 0), 40, 1)
        v3[x, :, 0:128] = jnp.where(lane < 84, before, here).astype(BF)
        v3[x, :, 128:256] = jnp.where(lane < 40, here, after).astype(BF)

    def mask_of(x, lo, size):
        m = masks[x, lo : lo + size]
        return jnp.concatenate([m, m], axis=1)

    def first_weights(turn):
        for a in range(3):
            total = None
            for b in range(3):
                w = win_ref[2 - a, 2 - b] if turn else win_ref[a, b]
                term = dot((iota((256, 84), 0) == iota((256, 84), 1) + 84 * b).astype(BF), w)
                total = term if total is None else total + term
            w1_ref[a] = total.astype(BF)

    copies[0].wait()
    first_weights(False)
    chunk = 5
    for c0 in range(0, n1, chunk):
        acc = None
        for a in range(3):
            d = dot(v3[c0 + a : c0 + a + chunk].reshape(chunk * PITCH, 256), w1_ref[a])
            acc = d if acc is None else acc + d
        acc = acc.reshape(chunk, PITCH, 256)
        for k in range(chunk):
            x = c0 + k
            g = gelu(acc[k]) * mask_of(x + 1, 0, PITCH)
            h3[x, :, 0:256] = pltpu.roll(g, 1, 0).astype(BF)
            h3[x, :, 256:512] = g.astype(BF)
            h3[x, :, 512:768] = pltpu.roll(g, PITCH - 1, 0).astype(BF)

    @pl.when(top)
    def _():
        first_weights(True)
        acc = None
        for a in range(3):
            d = dot(v3[a : a + n1, 128:144, :].reshape(n1 * 16, 256), w1_ref[a])
            acc = d if acc is None else acc + d
        acc = acc.reshape(n1, 16, 256)
        row = iota((16, 256), 0)
        for x in range(n1):
            g = gelu(acc[x]) * mask_of(x + 1, 128, 16)
            old = h3[x, 128:144, 256:512].astype(F32)
            new = jnp.where((row == 8) | (row == 9), g, old)
            h3[x, 128:144, 256:512] = new.astype(BF)
            old = h3[x, 128:144, 0:256].astype(F32)
            h3[x, 128:144, 0:256] = jnp.where((row == 9) | (row == 10), pltpu.roll(new, 1, 0), old).astype(BF)
            old = h3[x, 128:144, 512:768].astype(F32)
            h3[x, 128:144, 512:768] = jnp.where((row == 7) | (row == 8), pltpu.roll(new, 15, 0), old).astype(BF)

    copies[1].wait()
    chunk = 6
    for c0 in range(0, n2, chunk):
        acc = None
        for a in range(3):
            d = dot(h3[c0 + a : c0 + a + chunk].reshape(chunk * PITCH, 768), w2_ref[a])
            acc = d if acc is None else acc + d
        acc = acc.reshape(chunk, PITCH, 256)
        for k in range(chunk):
            x = c0 + k
            h2[x] = (gelu(acc[k]) * mask_of(x + 2, 0, PITCH)).astype(BF)

    @pl.when(top)
    def _():
        acc = None
        for a in range(3):
            for b in range(3):
                lhs = h3[a : a + n2, 128:144, 256 * b : 256 * b + 256].reshape(n2 * 16, 256)
                d = dot(lhs, w2_ref[2 - a, 256 * (2 - b) : 256 * (2 - b) + 256, :])
                acc = d if acc is None else acc + d
        acc = acc.reshape(n2, 16, 256)
        row = iota((16, 256), 0)
        for x in range(n2):
            g = gelu(acc[x]) * mask_of(x + 2, 128, 16)
            old = h2[x, 128:144].astype(F32)
            h2[x, 128:144] = jnp.where(row == 8, g, old).astype(BF)

    copies[2].wait()
    for a in range(3):
        for b in range(3):
            w = wout_ref[a, b].astype(F32)
            w3_ref[a, 128 * b : 128 * b + 128] = jnp.concatenate([w, jnp.zeros((52, 256), F32)], axis=0).astype(BF)
    chunk = 4
    for c0 in range(0, n3, chunk):
        acc = None
        for a in range(3):
            d = dot_nt(h2[c0 + a : c0 + a + chunk].reshape(chunk * PITCH, 256), w3_ref[a])
            acc = d if acc is None else acc + d
        acc = acc.reshape(chunk, PITCH, 384)
        for k in range(chunk):
            x = c0 + k
            change = (
                pltpu.roll(acc[k][:, 0:128], 1, 0)
                + acc[k][:, 128:256]
                + pltpu.roll(acc[k][:, 256:384], PITCH - 1, 0)
            )[8:136]
            new = (state_ref[x].astype(F32) + change) * masks[x + 3, 8:136]
            result[:, x, :] = new.T[:80]
    out_ref[...] = result[...][:76].astype(BF)


def convolutions(*args):
    return pl.pallas_call(
        conv_kernel,
        in_specs=[smem_spec()] + vmem_specs(len(args) - 4) + hbm_specs(3),
        out_specs=vmem_specs(1)[0],
        out_shape=jax.ShapeDtypeStruct((76, 16, 128), BF),
        scratch_shapes=[
            pltpu.VMEM((22, PITCH, 256), BF),
            pltpu.VMEM((20, PITCH, 768), BF),
            pltpu.VMEM((18, PITCH, 256), BF),
            pltpu.VMEM((80, 16, 128), F32),
            pltpu.VMEM((22, PITCH, 128), F32),
        ]
        + [pltpu.VMEM(w.shape, BF) for w in args[-3:]]
        + [
            pltpu.VMEM((3, 256, 256), BF),
            pltpu.VMEM((3, 384, 256), BF),
            pltpu.SemaphoreType.DMA((3,)),
        ],
        compiler_params=params(32),
        cost_estimate=pl.CostEstimate(flops=8 * 10**9, bytes_accessed=8 * 10**6, transcendentals=0),
        name="convolutions",
    )(*args[:-3], *in_hbm(*args[-3:]))


def shifted(forth, back, axis, periodic):
    count = lax.axis_size(axis)
    forward = [(i, i + 1) for i in range(count - 1)]
    if periodic:
        forward.append((count - 1, 0))
    backward = [(b, a) for a, b in forward]
    return lax.ppermute(forth, axis, forward), lax.ppermute(back, axis, backward)


def turned(x, axis, by):
    count = lax.axis_size(axis)
    return lax.ppermute(x, axis, [(i, (i + by) % count) for i in range(count)])


def per_tile(x, groups=None):
    return lax.all_to_all(x, "tile", split_axis=0, concat_axis=0, tiled=True, axis_index_groups=groups)


def per_device(
    atm_state,
    surface,
    mlp_in,
    mlp_mid,
    mlp_out,
    mlp_flux,
    ocean_state,
    ocean_mask,
    fold_map,
    pair_tile,
    pair_block,
    pair_count,
    margin,
    conv_in,
    conv_mid,
    conv_out,
):
    lev_dev = atm_state.shape[0]
    groups = lax.axis_size("lev")
    tiles = lax.axis_size("tile")
    _, span_x, span_y = ocean_state.shape
    pairs, blk = margin.shape[0], margin.shape[1]
    along_z = [[(x * ZS + z) * CS + c for z in range(ZS)] for x in range(tiles // (ZS * CS)) for c in range(CS)]
    same_z = [[(x * ZS + z) * CS + c for x in range(tiles // (ZS * CS)) for c in range(CS)] for z in range(ZS)]

    pieces = collect(atm_state, surface, groups)
    *pieces, tile_of, state_in = lax.optimization_barrier((*pieces, pair_tile, ocean_state))
    pieces = [pieces[0]] + [turned(pieces[k], "lev", k) for k in range(1, groups)]

    def across(asks, bit):
        return lax.ppermute(asks, "tile", [(t, t ^ (CS * bit)) for t in range(tiles)])

    asks, seam = asking(tile_of, pair_block, pair_count, fold_map)
    asks = jnp.concatenate([asks, across(asks, 1)], axis=0)

    state, *weights = prepare(state_in, ocean_mask, mlp_in, mlp_mid, mlp_out.T, mlp_flux.T)

    state, asks = lax.optimization_barrier((state, asks))
    *updated, send = column_model(pieces, *weights, state)
    near = jnp.concatenate([asks, across(asks, 2)], axis=0)
    blocks = per_tile(send, same_z)
    got = per_tile(pack(seam, near, across(near, 4), blocks), along_z)

    back = [updated[0]] + [turned(updated[k], "lev", -k) for k in range(1, groups)]
    atm_next = spread(back, lev_dev)
    above, below = back[1], back[3]

    flux, last, first, top, partner = remap(
        seam, got, margin.reshape(pairs * blk * span_x, span_y), state, below, above, tiles
    )

    low, high = shifted(last, first, "tile", True)
    tops = per_tile(top)
    wide, up, down = rim(low, flux, high)
    south, north = shifted(up, down, "lev", False)
    ocean_next = convolutions(
        seam, state, below, above, low, high, partner, wide, south, north, tops,
        conv_in, conv_mid.reshape(3, 768, 256), conv_out.transpose(0, 1, 3, 2),
    )
    return (atm_next, ocean_next)


def solution(mesh):
    return jax.shard_map(
        per_device,
        mesh=mesh,
        in_specs=(
            P("lev", None, "tile"),
            P("lev", "tile"),
            P(),
            P(),
            P(),
            P(),
            P(None, "tile", "lev"),
            P("tile", "lev"),
            P(),
            P("tile", "lev", None),
            P("tile", "lev", None),
            P("tile", "lev"),
            P(None, None, "tile", "lev"),
            P(),
            P(),
            P(),
        ),
        out_specs=(P("lev", None, "tile"), P(None, "tile", "lev")),
        check_vma=False,
    )
```

```python
import jax
import jax.numpy as jnp
from jax import lax
from jax.experimental import pallas as pl
from jax.experimental.pallas import tpu as pltpu
from jax.sharding import PartitionSpec as P

BF = jnp.bfloat16
F32 = jnp.float32
I32 = jnp.int32
SLAB = 8
HALO = 3
ZS, CS = 8, 2
PITCH = 144
LANES = 128
MIB = 1024 * 1024
C1 = 0.7978845608028654
C2 = C1 * 0.044715


def gelu(x):
    half = 0.5 * x
    return half * jnp.tanh(x * (C1 + C2 * (x * x))) + half


def dot(a, b):
    return jnp.dot(a, b, preferred_element_type=F32)


def dot_nt(a, b):
    return lax.dot_general(a, b, (((1,), (1,)), ((), ())), preferred_element_type=F32)


def iota(shape, dim):
    return lax.broadcasted_iota(I32, shape, dim)


def vmem_specs(n):
    return [pl.BlockSpec(memory_space=pltpu.VMEM)] * n


def hbm_specs(n):
    return [pl.BlockSpec(memory_space=pltpu.HBM)] * n


def in_hbm(*arrays):
    return [pltpu.with_memory_space_constraint(x, pltpu.HBM) for x in arrays]


def fetch(pairs, sems):
    copies = [pltpu.make_async_copy(a, b, sems.at[i]) for i, (a, b) in enumerate(pairs)]
    for copy in copies:
        copy.start()
    return copies


def smem_spec():
    return pl.BlockSpec(memory_space=pltpu.SMEM)


def params(mib):
    return pltpu.CompilerParams(vmem_limit_bytes=mib * MIB)


def place():
    tile = lax.axis_index("tile")
    return tile, lax.rem(tile // CS, ZS)


def collect_kernel(atm_ref, surface_ref, *refs):
    *out_refs, atm, surface, sems = refs
    levels, _, cols = atm_ref.shape
    parts = len(out_refs)
    size = cols // parts
    lev = lax.axis_index("lev")
    zero = jnp.zeros((1, size), F32)
    spans = [pl.ds(pl.multiple_of(lax.rem(lev + k, parts) * size, size), size) for k in range(parts)]
    order = (1, 2, 3, 0)
    copies = fetch([(surface_ref, surface)] + [(atm_ref.at[:, :, spans[k]], atm.at[k]) for k in order], sems)
    copies[0].wait()
    for i, k in enumerate(order):
        copies[1 + i].wait()
        rows = []
        for j in range(levels):
            extra = surface[:, spans[k]].astype(F32) if j == 0 else zero
            rows += [atm[k, j].astype(F32), extra, zero]
        out_refs[k][...] = jnp.concatenate(rows, axis=0).astype(BF)


def collect(atm, surface, parts):
    levels, _, cols = atm.shape
    return pl.pallas_call(
        collect_kernel,
        in_specs=hbm_specs(2),
        out_specs=vmem_specs(parts),
        out_shape=[jax.ShapeDtypeStruct((levels * SLAB, cols // parts), BF)] * parts,
        scratch_shapes=[
            pltpu.VMEM((parts, levels, 6, cols // parts), BF),
            pltpu.VMEM((1, cols), BF),
            pltpu.SemaphoreType.DMA((parts + 1,)),
        ],
        compiler_params=params(8),
        cost_estimate=pl.CostEstimate(flops=10**6, bytes_accessed=10**6, transcendentals=0),
        name="collect",
    )(*in_hbm(atm, surface))


def spread_kernel(*refs):
    back_refs, out_ref = refs[:-1], refs[-1]
    parts, size = len(back_refs), back_refs[0].shape[1]
    lev = lax.axis_index("lev")
    for k in range(parts):
        rows = back_refs[k][...].astype(F32)
        span = pl.ds(pl.multiple_of(lax.rem(lev + k, parts) * size, size), size)
        for j in range(out_ref.shape[0]):
            out_ref[j, :, span] = rows[SLAB * j : SLAB * j + 6].astype(BF)


def spread(back, levels):
    parts, size = len(back), back[0].shape[1]
    return pl.pallas_call(
        spread_kernel,
        in_specs=vmem_specs(parts),
        out_specs=vmem_specs(1)[0],
        out_shape=jax.ShapeDtypeStruct((levels, 6, parts * size), BF),
        compiler_params=params(8),
        cost_estimate=pl.CostEstimate(flops=10**6, bytes_accessed=10**6, transcendentals=0),
        name="spread",
    )(*back)


def asking_kernel(count_ref, tile_in, block_in, fold_in, out_ref, seam_ref, tile_ref, block_ref, fold_ref, sems):
    pairs = [(tile_in, tile_ref), (block_in, block_ref), (fold_in, fold_ref)]
    for copy in fetch(pairs, sems):
        copy.wait()
    seam_ref[0] = fold_ref[0]
    for p in range(4):
        seam_ref[1 + p] = tile_ref[0, 0, p]
    seam_ref[5] = count_ref[0, 0]
    rows, zs = [], []
    for p in range(4):
        source, block = tile_ref[0, 0, p], block_ref[0, 0, p]
        number = (source // (CS * ZS) * CS + lax.rem(source, CS)) * 16 + block
        z = jnp.where(p < count_ref[0, 0], lax.rem(source // CS, ZS), -1)
        rows.append(jnp.full((1, 128), number, I32))
        zs.append(jnp.full((1, 128), z, I32))
    out_ref[0] = jnp.concatenate(rows + zs + [jnp.zeros((8, 128), I32)], axis=0).astype(F32).astype(BF)


def asking(tile, block, count, fold_map):
    return pl.pallas_call(
        asking_kernel,
        in_specs=[smem_spec()] + hbm_specs(3),
        out_specs=vmem_specs(1) + [smem_spec()],
        out_shape=[jax.ShapeDtypeStruct((1, 16, 128), BF), jax.ShapeDtypeStruct((8,), I32)],
        scratch_shapes=[pltpu.SMEM(x.shape, I32) for x in (tile, block, fold_map)]
        + [pltpu.SemaphoreType.DMA((3,))],
        compiler_params=params(4),
        cost_estimate=pl.CostEstimate(flops=10**6, bytes_accessed=10**5, transcendentals=0),
        name="asking",
    )(count, *in_hbm(tile, block, fold_map))


def prepare_kernel(
    state_in, mask_in, win_in, wmid_in, wout_in, wflux_in, state_ref, w1_ref, w2_ref, w3_ref,
    state, mask_ref, win_ref, wmid_ref, wout_ref, wflux_ref, rows, sems,
):
    copies = fetch(
        [
            (state_in, state), (mask_in, mask_ref), (win_in, win_ref), (wmid_in, wmid_ref), (wout_in, wout_ref),
            (wflux_in, wflux_ref),
        ],
        sems,
    )
    channels, cols, size = state_in.shape
    copies[0].wait()
    copies[1].wait()
    rows[...] = state[...].reshape(channels * cols, size).astype(F32)
    for x in range(cols):
        part = rows[pl.ds(x, channels, stride=cols), :]
        mask = mask_ref[x : x + 1].astype(F32)
        part = jnp.concatenate(
            [part, jnp.zeros((84 - channels, size), F32), mask, jnp.zeros((LANES - 85, size), F32)], axis=0
        )
        state_ref[x] = part.T.astype(BF)
    for copy in copies[2:]:
        copy.wait()
    lev = lax.axis_index("lev")
    rows_all = w1_ref.shape[1]
    size = rows_all // 4

    def origin(shape):
        row = iota(shape, 0)
        group = (lev - row // size) & 3
        level, field = 3 * group + row % size // 8, row % 8
        return jnp.where((field < 6) & (row < rows_all), 6 * level + field, -1), group, row

    source, group, row = origin((rows_all, 76))
    source = jnp.where(row % size == 6, 72 + group, source)
    w1_ref[...] = dot((iota((rows_all, 76), 1) == source).astype(BF), win_ref[...]).T.astype(BF)
    source, group, row = origin((rows_all + 8, 72))
    w3 = dot((iota((rows_all + 8, 72), 1) == source).astype(BF), wout_ref[...])
    w3 = w3 + dot((iota((rows_all + 8, 8), 1) == iota((rows_all + 8, 8), 0) - rows_all).astype(BF), wflux_ref[...])
    w3_ref[...] = w3.astype(BF)
    w2_ref[...] = wmid_ref[...].T


def prepare(state, mask, *weights):
    channels, cols, size = state.shape
    hid = weights[1].shape[0]
    return pl.pallas_call(
        prepare_kernel,
        in_specs=hbm_specs(6),
        out_specs=vmem_specs(4),
        out_shape=[
            jax.ShapeDtypeStruct((cols, size, LANES), BF),
            jax.ShapeDtypeStruct((hid, 96), BF),
            jax.ShapeDtypeStruct((hid, hid), BF),
            jax.ShapeDtypeStruct((104, hid), BF),
        ],
        scratch_shapes=[pltpu.VMEM(state.shape, BF), pltpu.VMEM(mask.shape, I32)]
        + [pltpu.VMEM(w.shape, BF) for w in weights]
        + [pltpu.VMEM((channels * cols, size), F32), pltpu.SemaphoreType.DMA((6,))],
        compiler_params=params(12),
        cost_estimate=pl.CostEstimate(flops=10**9, bytes_accessed=10**6, transcendentals=0),
        name="prepare",
    )(*in_hbm(state, mask, *weights))


def mlp_kernel(z0_ref, z1_ref, z2_ref, z3_ref, w1_ref, w2_ref, w3_ref, state_ref, *out_refs):
    z_refs, up_refs, send_ref = (z0_ref, z1_ref, z2_ref, z3_ref), out_refs[:4], out_refs[4]
    size, cols = z0_ref.shape
    rows = 4 * size
    step = 512
    w1, w2, w3 = w1_ref[...], w2_ref[...], w3_ref[...]
    for c in range(0, cols, step):
        z = jnp.concatenate([ref[:, c : c + step].astype(F32) for ref in z_refs], axis=0)
        first = gelu(dot(w1, z.astype(BF))).astype(BF)
        second = gelu(dot(w2, first)).astype(BF)
        out = dot(w3, second)
        for k in range(4):
            span = slice(size * k, size * k + size)
            up = z[span] + out[span]
            if k == 1 or k == 3:
                rim = []
                for x in range(c // 128, (c + step) // 128):
                    tile = state_ref[x, 0:16] if k == 1 else state_ref[x, 112:128]
                    rim.append(tile.astype(F32)[:8] if k == 1 else tile.astype(F32)[8:])
                up = jnp.concatenate([up, jnp.concatenate(rim, axis=1)], axis=0)
            up_refs[k][:, c : c + step] = up.astype(BF)
        for k in range(0, step, 256):
            both = jnp.concatenate([out[rows : rows + 8, k : k + 128], out[rows : rows + 8, k + 128 : k + 256]], axis=0)
            send_ref[0, (c + k) // 256] = both.astype(BF)
    row, col = iota((48, 256), 0), iota((48, 256), 1)
    pick = (col == row // 3 * 16 + 13 + row % 3).astype(BF)
    strip = dot(pick, state_ref[:, 112:128].reshape(256, 128)).astype(BF)
    send_ref[0, 8:11] = strip.reshape(3, 16, 128)
    for j in range(1, send_ref.shape[0]):
        send_ref[j] = send_ref[0]


def column_model(pieces, w1, w2, w3, state):
    size, cols = pieces[0].shape
    return pl.pallas_call(
        mlp_kernel,
        in_specs=vmem_specs(8),
        out_specs=vmem_specs(5),
        out_shape=[
            jax.ShapeDtypeStruct((size, cols), BF),
            jax.ShapeDtypeStruct((size + 8, cols), BF),
            jax.ShapeDtypeStruct((size, cols), BF),
            jax.ShapeDtypeStruct((size + 8, cols), BF),
            jax.ShapeDtypeStruct((8, 11, 16, 128), BF),
        ],
        compiler_params=params(20),
        cost_estimate=pl.CostEstimate(flops=3 * 10**9, bytes_accessed=2 * 10**6, transcendentals=0),
        name="column_model",
    )(*pieces, w1, w2, w3, state)


def pack_kernel(seam_ref, near_ref, far_ref, got_ref, send_ref):
    tile, z_me = place()
    number, zs = [], []
    for m in range(ZS):
        ask = (near_ref if m < 4 else far_ref)[m % 4].astype(F32).astype(I32)
        for p in range(4):
            number.append(jnp.broadcast_to(ask[p : p + 1], (8, 128)))
            zs.append(jnp.broadcast_to(ask[4 + p : 5 + p], (8, 128)))
    number, zs = jnp.concatenate(number, axis=0), jnp.concatenate(zs, axis=0)
    wanted = jnp.where(zs == z_me, number * 8 + iota((256, 128), 0) % 8, -1)
    total = None
    for j in range(8):
        pick = (wanted == iota((256, 128), 1) + 128 * j).astype(BF)
        term = dot(pick, got_ref[j, 0:8].reshape(128, 128))
        total = term if total is None else total + term
    total = total.astype(BF).reshape(ZS, 2, 16, 128)
    for m in range(ZS):
        send_ref[ZS - 1 - (z_me ^ m), 0:2] = total[m]
    key = (seam_ref[0] + HALO) // 16 - 1 + 128
    core = lax.rem(tile, CS)
    z_to = lax.rem(key - lax.rem(key - core, CS) - CS * z_me, CS * ZS) // CS
    source = lax.rem(key - (tile - CS * z_me + CS * z_to), 64)
    strip = got_ref[source // (CS * ZS) * CS + lax.rem(source, CS), 8:11]
    for z in range(ZS):
        send_ref[z, 2:5] = strip


def pack(seam, near, far, got):
    return pl.pallas_call(
        pack_kernel,
        in_specs=[smem_spec()] + vmem_specs(3),
        out_specs=vmem_specs(1)[0],
        out_shape=jax.ShapeDtypeStruct((ZS, 5, 16, 128), BF),
        compiler_params=params(8),
        cost_estimate=pl.CostEstimate(flops=10**8, bytes_accessed=10**6, transcendentals=0),
        name="pack",
    )(seam, near, far, got)


def tall(state_ref, south_ref, north_ref, x):
    size = south_ref.shape[0] - 8
    lanes = slice(LANES * x, LANES * x + LANES)
    south = jnp.where(lax.axis_index("lev") > 0, south_ref[:, lanes].astype(F32)[size:], 0.0)
    return jnp.concatenate([south, state_ref[x].astype(F32), north_ref[:, lanes].astype(F32)[size:]], axis=0)


def remap_kernel(
    seam_ref, got_ref, margin_ref, state_ref, south_ref, north_ref,
    flux_ref, east_ref, west_ref, top_ref, strip_ref,
):
    partner = lax.rem((seam_ref[0] + HALO) // 16 - 1 - lax.axis_index("tile") + 128, 64)
    strip = got_ref[ZS - 1 - lax.rem(partner // CS, ZS), 2:5]
    strip_ref[...] = strip
    for side_ref, x in ((east_ref, 13), (west_ref, 0)):
        for k in range(HALO):
            side_ref[PITCH * k : PITCH * k + PITCH] = tall(state_ref, south_ref, north_ref, x + k).astype(BF)
        side_ref[432:480] = strip.reshape(48, 128)
    count = seam_ref[5]
    pieces = []
    for p in range(4):
        source = jnp.clip(seam_ref[1 + p], 0, 63)
        piece = got_ref[ZS - 1 - lax.rem(source // CS, ZS), p // 2].astype(F32)[8 * (p % 2) : 8 * (p % 2) + 8]
        pieces.append(jnp.where(p < count, piece, 0.0))
    blocks = jnp.concatenate(pieces, axis=0).astype(BF)
    spread = (iota((128, 2048), 0) == iota((128, 2048), 1) // 16).astype(BF)
    wide = dot(blocks, spread)
    same = iota((16, 2048), 0) == iota((16, 2048), 1) % 16
    total = None
    for p in range(4):
        rows = jnp.broadcast_to(wide[8 * p : 8 * p + 8][None], (16, 8, 2048))
        rows = jnp.where(same[:, None, :], rows, 0.0).reshape(128, 2048)
        ones = jnp.where(same & (p < count), 1.0, 0.0)
        left = jnp.concatenate([rows, ones], axis=0).astype(BF)
        term = dot(left, margin_ref[2048 * p : 2048 * p + 2048])
        total = term if total is None else total + term
    numer = total[:128].reshape(16, 8, 128)
    flux = (numer / total[128:144][:, None, :]).reshape(128, 128).astype(BF)
    flux_ref[...] = flux
    wide = flux.astype(F32)
    zero = jnp.zeros((8, 128), F32)
    east_ref[480:512] = jnp.concatenate([wide[104:128], zero], axis=0).astype(BF)
    west_ref[480:512] = jnp.concatenate([wide[0:24], zero], axis=0).astype(BF)
    top = dot_nt((iota((8, 128), 1) == 127 - iota((8, 128), 0)).astype(BF), flux).astype(BF)
    top_ref[...] = jnp.broadcast_to(top[None], top_ref.shape)


def remap(seam, got, margin, state, south, north, tiles):
    side = jax.ShapeDtypeStruct((512, 128), BF)
    return pl.pallas_call(
        remap_kernel,
        in_specs=[smem_spec()] + vmem_specs(5),
        out_specs=vmem_specs(5),
        out_shape=[
            jax.ShapeDtypeStruct((128, 128), BF),
            side,
            side,
            jax.ShapeDtypeStruct((tiles, 8, 128), BF),
            jax.ShapeDtypeStruct((3, 16, 128), BF),
        ],
        compiler_params=params(16),
        cost_estimate=pl.CostEstimate(flops=10**9, bytes_accessed=3 * 10**6, transcendentals=0),
        name="remap",
    )(seam, got, margin, state, south, north)


def rim_kernel(low_ref, flux_ref, high_ref, wide_ref, up_ref, down_ref):
    low, high = low_ref[480:512].astype(F32)[:24], high_ref[480:512].astype(F32)[:24]
    wide = jnp.concatenate([low, flux_ref[...].astype(F32), high, jnp.zeros((80, 128), F32)], axis=0).astype(BF)
    wide_ref[...] = wide
    row, col = iota((16, 128), 0), iota((16, 128), 1)
    up_ref[...] = dot_nt(((col == 125 + row) & (row < 3)).astype(BF), wide).astype(BF)
    down_ref[...] = dot_nt(((col == row) & (row < 3)).astype(BF), wide).astype(BF)


def rim(low, flux, high):
    strip = jax.ShapeDtypeStruct((16, 256), BF)
    return pl.pallas_call(
        rim_kernel,
        in_specs=vmem_specs(3),
        out_specs=vmem_specs(3),
        out_shape=[jax.ShapeDtypeStruct((256, 128), BF), strip, strip],
        compiler_params=params(4),
        cost_estimate=pl.CostEstimate(flops=10**8, bytes_accessed=10**6, transcendentals=0),
        name="rim",
    )(low, flux, high)


def conv_kernel(
    seam_ref, state_ref, below_ref, above_ref, west_ref, east_ref, strip_ref, wide_ref, south_ref, north_ref, tops_ref,
    w1_ref, w1r_ref, w3_ref, wmid_in, out_ref, v3, h3, h2, result, masks, w2_ref, sems,
):
    copies = fetch([(wmid_in, w2_ref)], sems)
    tiles = tops_ref.shape[0]
    tile = lax.axis_index("tile")
    top = lax.axis_index("lev") == lax.axis_size("lev") - 1
    n0, n1, n2, n3 = 22, 20, 18, 16
    seam = (seam_ref[0] + HALO) // 16
    shift = lax.rem(seam_ref[0] + HALO, 16)

    u, f = iota((128, 256), 0) // 8, iota((128, 256), 0) % 8
    i, g = iota((128, 256), 1) // 8, iota((128, 256), 1) % 8
    fold = None
    for e in range(3):
        pick = ((f == g) & (u == 16 * e + shift - i)).astype(BF)
        part = tops_ref[tiles - 1 - lax.rem(seam - tile - e + 2 * tiles, tiles)].astype(F32)
        term = dot(jnp.concatenate([part, jnp.zeros((8, 128), F32)], axis=0).astype(BF), pick)
        fold = term if fold is None else fold + term
    strips = jnp.concatenate(
        [west_ref[432:480], strip_ref[...].reshape(48, 128), east_ref[432:480]], axis=0
    )
    i, k = iota((352, 144), 0) // 16, iota((352, 144), 0) % 16 - 8
    e, u, r = iota((352, 144), 1) // 48, iota((352, 144), 1) % 48 // 3, iota((352, 144), 1) % 3
    folded = dot(((u == 16 * e + shift - i) & (r == 2 - k) & (k >= 0) & (k < 3)).astype(BF), strips)
    over = iota((16, LANES), 0)
    over = top & (over >= 8) & (over < 11)

    def state_of(x):
        if x < 3:
            v = west_ref[PITCH * x : PITCH * x + PITCH].astype(F32)
        elif x < 19:
            v = tall(state_ref, below_ref, above_ref, x - 3)
        else:
            v = east_ref[PITCH * (x - 19) : PITCH * (x - 19) + PITCH].astype(F32)
        return jnp.concatenate([v[:128], jnp.where(over, folded[16 * x : 16 * x + 16], v[128:])], axis=0)

    north = jnp.where(top, fold, north_ref[...].astype(F32))
    rims = jnp.concatenate([south_ref[...].astype(F32), north], axis=0).astype(BF)
    row, col = iota((PITCH, 128), 0), iota((PITCH, 128), 1)
    fluxes = dot_nt((row == col + 8).astype(BF), wide_ref[...])
    row, col = iota((PITCH, 32), 0), iota((PITCH, 32), 1)
    put = ((col < 3) & (row == col + 5)) | ((col >= 16) & (col < 19) & (row == col - 16 + 136))
    fluxes = fluxes + dot(put.astype(BF), rims)
    lane = iota((PITCH, LANES), 1)

    for x in range(n0):
        start = 8 * x
        part = fluxes[:, 128 * (start // 128) : 128 * (start // 128) + 128]
        part = pltpu.roll(part, (76 - start) % 128, 1)
        state = state_of(x)
        masks[x] = jnp.broadcast_to(state[:, 84:85], (PITCH, 128))
        v = jnp.where(lane < 76, state, jnp.where(lane < 84, part, 0.0))
        before = pltpu.roll(v, 1, 0)
        here = pltpu.roll(v, 84, 1)
        after = pltpu.roll(pltpu.roll(v, PITCH - 1, 0), 40, 1)
        v3[x, :, 0:128] = jnp.where(lane < 84, before, here).astype(BF)
        v3[x, :, 128:256] = jnp.where(lane < 40, here, after).astype(BF)

    def mask_of(x, lo, size):
        m = masks[x, lo : lo + size]
        return jnp.concatenate([m, m], axis=1)

    chunk = 2
    for c0 in range(0, n1, chunk):
        left = jnp.concatenate([v3[c0 + a : c0 + a + chunk].reshape(chunk * PITCH, 256) for a in range(3)], axis=1)
        acc = dot(left, w1_ref[...].reshape(768, 256))
        acc = acc.reshape(chunk, PITCH, 256)
        for k in range(chunk):
            x = c0 + k
            g = gelu(acc[k]) * mask_of(x + 1, 0, PITCH)
            h3[x, :, 0:256] = pltpu.roll(g, 1, 0).astype(BF)
            h3[x, :, 256:512] = g.astype(BF)
            h3[x, :, 512:768] = pltpu.roll(g, PITCH - 1, 0).astype(BF)

    @pl.when(top)
    def _():
        acc = None
        for a in range(3):
            d = dot(v3[a : a + n1, 128:144, :].reshape(n1 * 16, 256), w1r_ref[a])
            acc = d if acc is None else acc + d
        acc = acc.reshape(n1, 16, 256)
        row = iota((16, 256), 0)
        for x in range(n1):
            g = gelu(acc[x]) * mask_of(x + 1, 128, 16)
            old = h3[x, 128:144, 256:512].astype(F32)
            new = jnp.where((row == 8) | (row == 9), g, old)
            h3[x, 128:144, 256:512] = new.astype(BF)
            old = h3[x, 128:144, 0:256].astype(F32)
            h3[x, 128:144, 0:256] = jnp.where((row == 9) | (row == 10), pltpu.roll(new, 1, 0), old).astype(BF)
            old = h3[x, 128:144, 512:768].astype(F32)
            h3[x, 128:144, 512:768] = jnp.where((row == 7) | (row == 8), pltpu.roll(new, 15, 0), old).astype(BF)

    copies[0].wait()
    chunk = 2
    for c0 in range(0, n2, chunk):
        left = jnp.concatenate([h3[c0 + a : c0 + a + chunk].reshape(chunk * PITCH, 768) for a in range(3)], axis=1)
        acc = dot(left, w2_ref[...].reshape(2304, 256))
        acc = acc.reshape(chunk, PITCH, 256)
        for k in range(chunk):
            x = c0 + k
            h2[x] = (gelu(acc[k]) * mask_of(x + 2, 0, PITCH)).astype(BF)

    @pl.when(top)
    def _():
        acc = None
        for a in range(3):
            for b in range(3):
                lhs = h3[a : a + n2, 128:144, 256 * b : 256 * b + 256].reshape(n2 * 16, 256)
                d = dot(lhs, w2_ref[2 - a, 256 * (2 - b) : 256 * (2 - b) + 256, :])
                acc = d if acc is None else acc + d
        acc = acc.reshape(n2, 16, 256)
        row = iota((16, 256), 0)
        for x in range(n2):
            g = gelu(acc[x]) * mask_of(x + 2, 128, 16)
            old = h2[x, 128:144].astype(F32)
            h2[x, 128:144] = jnp.where(row == 8, g, old).astype(BF)

    chunk = 2
    for c0 in range(0, n3, chunk):
        left = jnp.concatenate([h2[c0 + a : c0 + a + chunk].reshape(chunk * PITCH, 256) for a in range(3)], axis=1)
        acc = dot_nt(left, w3_ref[...])
        acc = acc.reshape(chunk, PITCH, 384)
        for k in range(chunk):
            x = c0 + k
            change = (
                pltpu.roll(acc[k][:, 0:128], 1, 0)
                + acc[k][:, 128:256]
                + pltpu.roll(acc[k][:, 256:384], PITCH - 1, 0)
            )[8:136]
            new = (state_ref[x].astype(F32) + change) * masks[x + 3, 8:136]
            result[:, x, :] = new.T[:80]
    out_ref[...] = result[...][:76].astype(BF)


def weights_kernel(flux_ref, win_in, wout_in, w1_ref, w1r_ref, w3_ref, win_ref, wout_ref, sems):
    copies = fetch([(win_in, win_ref), (wout_in, wout_ref)], sems)
    copies[0].wait()
    for ref, turn in ((w1_ref, False), (w1r_ref, True)):
        for a in range(3):
            total = None
            for b in range(3):
                w = win_ref[2 - a, 2 - b] if turn else win_ref[a, b]
                term = dot((iota((256, 84), 0) == iota((256, 84), 1) + 84 * b).astype(BF), w)
                total = term if total is None else total + term
            ref[a] = total.astype(BF)
    copies[1].wait()
    for a in range(3):
        for b in range(3):
            w = wout_ref[a, b].astype(F32)
            w = jnp.concatenate([w, jnp.zeros((52, 256), F32)], axis=0).astype(BF)
            w3_ref[128 * b : 128 * b + 128, 256 * a : 256 * a + 256] = w


def conv_weights(flux, win, wout):
    return pl.pallas_call(
        weights_kernel,
        in_specs=vmem_specs(1) + hbm_specs(2),
        out_specs=vmem_specs(3),
        out_shape=[
            jax.ShapeDtypeStruct((3, 256, 256), BF),
            jax.ShapeDtypeStruct((3, 256, 256), BF),
            jax.ShapeDtypeStruct((384, 768), BF),
        ],
        scratch_shapes=[pltpu.VMEM(w.shape, BF) for w in (win, wout)] + [pltpu.SemaphoreType.DMA((2,))],
        compiler_params=params(8),
        cost_estimate=pl.CostEstimate(flops=10**9, bytes_accessed=4 * 10**6, transcendentals=0),
        name="conv_weights",
    )(flux, *in_hbm(win, wout))


def convolutions(*args):
    return pl.pallas_call(
        conv_kernel,
        in_specs=[smem_spec()] + vmem_specs(len(args) - 2) + hbm_specs(1),
        out_specs=vmem_specs(1)[0],
        out_shape=jax.ShapeDtypeStruct((76, 16, 128), BF),
        scratch_shapes=[
            pltpu.VMEM((22, PITCH, 256), BF),
            pltpu.VMEM((20, PITCH, 768), BF),
            pltpu.VMEM((18, PITCH, 256), BF),
            pltpu.VMEM((80, 16, 128), F32),
            pltpu.VMEM((22, PITCH, 128), F32),
        ]
        + [pltpu.VMEM(args[-1].shape, BF), pltpu.SemaphoreType.DMA((1,))],
        compiler_params=params(24),
        cost_estimate=pl.CostEstimate(flops=8 * 10**9, bytes_accessed=8 * 10**6, transcendentals=0),
        name="convolutions",
    )(*args[:-1], *in_hbm(args[-1]))


def shifted(forth, back, axis, periodic):
    count = lax.axis_size(axis)
    forward = [(i, i + 1) for i in range(count - 1)]
    if periodic:
        forward.append((count - 1, 0))
    backward = [(b, a) for a, b in forward]
    return lax.ppermute(forth, axis, forward), lax.ppermute(back, axis, backward)


def turned(x, axis, by):
    count = lax.axis_size(axis)
    return lax.ppermute(x, axis, [(i, (i + by) % count) for i in range(count)])


def per_tile(x, groups=None):
    return lax.all_to_all(x, "tile", split_axis=0, concat_axis=0, tiled=True, axis_index_groups=groups)


def per_device(
    atm_state,
    surface,
    mlp_in,
    mlp_mid,
    mlp_out,
    mlp_flux,
    ocean_state,
    ocean_mask,
    fold_map,
    pair_tile,
    pair_block,
    pair_count,
    margin,
    conv_in,
    conv_mid,
    conv_out,
):
    lev_dev = atm_state.shape[0]
    groups = lax.axis_size("lev")
    tiles = lax.axis_size("tile")
    _, span_x, span_y = ocean_state.shape
    pairs, blk = margin.shape[0], margin.shape[1]
    along_z = [[(x * ZS + z) * CS + c for z in reversed(range(ZS))] for x in range(tiles // (ZS * CS)) for c in range(CS)]
    same_z = [[(x * ZS + z) * CS + c for x in range(tiles // (ZS * CS)) for c in range(CS)] for z in range(ZS)]

    pieces = collect(atm_state, surface, groups)
    *pieces, tile_of, state_in = lax.optimization_barrier((*pieces, pair_tile, ocean_state))
    pieces = [pieces[0]] + [turned(pieces[k], "lev", k) for k in range(1, groups)]

    def across(asks, bit):
        return lax.ppermute(asks, "tile", [(t, t ^ (CS * bit)) for t in range(tiles)])

    asks, seam = asking(tile_of, pair_block, pair_count, fold_map)
    asks = jnp.concatenate([asks, across(asks, 1)], axis=0)

    state, *weights = prepare(state_in, ocean_mask, mlp_in, mlp_mid, mlp_out.T, mlp_flux.T)

    state, asks = lax.optimization_barrier((state, asks))
    *updated, send = column_model(pieces, *weights, state)
    send, second = lax.optimization_barrier((send, across(asks, 2)))
    near = jnp.concatenate([asks, second], axis=0)
    blocks = per_tile(send, same_z)
    got = per_tile(pack(seam, near, across(near, 4), blocks), along_z)

    back = [updated[0]] + [turned(updated[k], "lev", -k) for k in range(1, groups)]
    atm_next = spread(back, lev_dev)
    above, below = back[1], back[3]

    flux, last, first, top, partner = remap(
        seam, got, margin.reshape(pairs * blk * span_x, span_y), state, below, above, tiles
    )

    low, high = shifted(last, first, "tile", True)
    tops = per_tile(top, [list(reversed(range(tiles)))])
    conv_ws = conv_weights(last, conv_in, conv_out.transpose(0, 1, 3, 2))
    low, high, *conv_ws = lax.optimization_barrier((low, high, *conv_ws))
    wide, up, down = rim(low, flux, high)
    south, north = shifted(up, down, "lev", False)
    ocean_next = convolutions(
        seam, state, below, above, low, high, partner, wide, south, north, tops,
        *conv_ws, conv_mid.reshape(3, 768, 256),
    )
    return (atm_next, ocean_next)


def solution(mesh):
    return jax.shard_map(
        per_device,
        mesh=mesh,
        in_specs=(
            P("lev", None, "tile"),
            P("lev", "tile"),
            P(),
            P(),
            P(),
            P(),
            P(None, "tile", "lev"),
            P("tile", "lev"),
            P(),
            P("tile", "lev", None),
            P("tile", "lev", None),
            P("tile", "lev"),
            P(None, None, "tile", "lev"),
            P(),
            P(),
            P(),
        ),
        out_specs=(P("lev", None, "tile"), P(None, "tile", "lev")),
        check_vma=False,
    )
```

```python
import jax
import jax.numpy as jnp
from jax import lax
from jax.experimental import pallas as pl
from jax.experimental.pallas import tpu as pltpu
from jax.sharding import PartitionSpec as P

BF = jnp.bfloat16
F32 = jnp.float32
I32 = jnp.int32
SLAB = 8
HALO = 3
ZS, CS = 8, 2
PITCH = 144
LANES = 128
MIB = 1024 * 1024
C1 = 0.7978845608028654
C2 = C1 * 0.044715


def gelu(x):
    half = 0.5 * x
    return half * jnp.tanh(x * (C1 + C2 * (x * x))) + half


def dot(a, b):
    return jnp.dot(a, b, preferred_element_type=F32)


def dot_nt(a, b):
    return lax.dot_general(a, b, (((1,), (1,)), ((), ())), preferred_element_type=F32)


def iota(shape, dim):
    return lax.broadcasted_iota(I32, shape, dim)


def vmem_specs(n):
    return [pl.BlockSpec(memory_space=pltpu.VMEM)] * n


def hbm_specs(n):
    return [pl.BlockSpec(memory_space=pltpu.HBM)] * n


def in_hbm(*arrays):
    return [pltpu.with_memory_space_constraint(x, pltpu.HBM) for x in arrays]


def fetch(pairs, sems):
    copies = [pltpu.make_async_copy(a, b, sems.at[i]) for i, (a, b) in enumerate(pairs)]
    for copy in copies:
        copy.start()
    return copies


def smem_spec():
    return pl.BlockSpec(memory_space=pltpu.SMEM)


def params(mib):
    return pltpu.CompilerParams(vmem_limit_bytes=mib * MIB)


def place():
    tile = lax.axis_index("tile")
    return tile, lax.rem(tile // CS, ZS)


def collect_kernel(count_ref, tile_in, block_in, fold_in, atm_ref, surface_ref, *refs):
    *out_refs, ask_ref, seam_ref, tile_ref, block_ref, fold_ref, atm, surface, sems = refs
    levels, _, cols = atm_ref.shape
    parts = len(out_refs)
    size = cols // parts
    lev = lax.axis_index("lev")
    zero = jnp.zeros((1, size), F32)
    spans = [pl.ds(pl.multiple_of(lax.rem(lev + k, parts) * size, size), size) for k in range(parts)]
    order = (1, 2, 3, 0)
    tables = [(tile_in, tile_ref), (block_in, block_ref), (fold_in, fold_ref)]
    copies = fetch(
        tables + [(surface_ref, surface)] + [(atm_ref.at[:, :, spans[k]], atm.at[k]) for k in order], sems
    )
    for copy in copies[:3]:
        copy.wait()
    seam_ref[0] = fold_ref[0]
    seam_ref[5] = count_ref[0, 0]
    rows, zs = [], []
    for p in range(4):
        source, block = tile_ref[0, 0, p], block_ref[0, 0, p]
        seam_ref[1 + p] = source
        number = (source // (CS * ZS) * CS + lax.rem(source, CS)) * 16 + block
        z = jnp.where(p < count_ref[0, 0], lax.rem(source // CS, ZS), -1)
        rows.append(jnp.full((1, 128), number, I32))
        zs.append(jnp.full((1, 128), z, I32))
    ask_ref[0] = jnp.concatenate(rows + zs + [jnp.zeros((8, 128), I32)], axis=0).astype(F32).astype(BF)
    copies[3].wait()
    for i, k in enumerate(order):
        copies[4 + i].wait()
        rows = []
        for j in range(levels):
            extra = surface[:, spans[k]].astype(F32) if j == 0 else zero
            rows += [atm[k, j].astype(F32), extra, zero]
        out_refs[k][...] = jnp.concatenate(rows, axis=0).astype(BF)


def collect(count, tile, block, fold_map, atm, surface, parts):
    levels, _, cols = atm.shape
    return pl.pallas_call(
        collect_kernel,
        in_specs=[smem_spec()] + hbm_specs(5),
        out_specs=vmem_specs(parts + 1) + [smem_spec()],
        out_shape=[jax.ShapeDtypeStruct((levels * SLAB, cols // parts), BF)] * parts
        + [jax.ShapeDtypeStruct((1, 16, 128), BF), jax.ShapeDtypeStruct((8,), I32)],
        scratch_shapes=[pltpu.SMEM(x.shape, I32) for x in (tile, block, fold_map)]
        + [
            pltpu.VMEM((parts, levels, 6, cols // parts), BF),
            pltpu.VMEM((1, cols), BF),
            pltpu.SemaphoreType.DMA((parts + 4,)),
        ],
        compiler_params=params(8),
        cost_estimate=pl.CostEstimate(flops=10**6, bytes_accessed=10**6, transcendentals=0),
        name="collect",
    )(count, *in_hbm(tile, block, fold_map, atm, surface))


def spread_kernel(*refs):
    back_refs, out_ref = refs[:-1], refs[-1]
    parts, size = len(back_refs), back_refs[0].shape[1]
    lev = lax.axis_index("lev")
    for k in range(parts):
        rows = back_refs[k][...].astype(F32)
        span = pl.ds(pl.multiple_of(lax.rem(lev + k, parts) * size, size), size)
        for j in range(out_ref.shape[0]):
            out_ref[j, :, span] = rows[SLAB * j : SLAB * j + 6].astype(BF)


def spread(back, levels):
    parts, size = len(back), back[0].shape[1]
    return pl.pallas_call(
        spread_kernel,
        in_specs=vmem_specs(parts),
        out_specs=vmem_specs(1)[0],
        out_shape=jax.ShapeDtypeStruct((levels, 6, parts * size), BF),
        compiler_params=params(8),
        cost_estimate=pl.CostEstimate(flops=10**6, bytes_accessed=10**6, transcendentals=0),
        name="spread",
    )(*back)


def prepare_kernel(
    state_in, mask_in, win_in, wmid_in, wout_in, wflux_in, state_ref, w1_ref, w2_ref, w3_ref,
    state, mask_ref, win_ref, wmid_ref, wout_ref, wflux_ref, rows, sems,
):
    copies = fetch(
        [
            (state_in, state), (mask_in, mask_ref), (win_in, win_ref), (wmid_in, wmid_ref), (wout_in, wout_ref),
            (wflux_in, wflux_ref),
        ],
        sems,
    )
    channels, cols, size = state_in.shape
    copies[0].wait()
    copies[1].wait()
    rows[...] = state[...].reshape(channels * cols, size).astype(F32)
    for x in range(cols):
        part = rows[pl.ds(x, channels, stride=cols), :]
        mask = mask_ref[x : x + 1].astype(F32)
        part = jnp.concatenate(
            [part, jnp.zeros((84 - channels, size), F32), mask, jnp.zeros((LANES - 85, size), F32)], axis=0
        )
        state_ref[x] = part.T.astype(BF)
    for copy in copies[2:]:
        copy.wait()
    lev = lax.axis_index("lev")
    rows_all = w1_ref.shape[1]
    size = rows_all // 4

    def origin(shape):
        row = iota(shape, 0)
        group = (lev - row // size) & 3
        level, field = 3 * group + row % size // 8, row % 8
        return jnp.where((field < 6) & (row < rows_all), 6 * level + field, -1), group, row

    source, group, row = origin((rows_all, 76))
    source = jnp.where(row % size == 6, 72 + group, source)
    w1_ref[...] = dot((iota((rows_all, 76), 1) == source).astype(BF), win_ref[...]).T.astype(BF)
    source, group, row = origin((rows_all + 8, 72))
    w3 = dot((iota((rows_all + 8, 72), 1) == source).astype(BF), wout_ref[...])
    w3 = w3 + dot((iota((rows_all + 8, 8), 1) == iota((rows_all + 8, 8), 0) - rows_all).astype(BF), wflux_ref[...])
    w3_ref[...] = w3.astype(BF)
    w2_ref[...] = wmid_ref[...].T


def prepare(state, mask, *weights):
    channels, cols, size = state.shape
    hid = weights[1].shape[0]
    return pl.pallas_call(
        prepare_kernel,
        in_specs=hbm_specs(6),
        out_specs=vmem_specs(4),
        out_shape=[
            jax.ShapeDtypeStruct((cols, size, LANES), BF),
            jax.ShapeDtypeStruct((hid, 96), BF),
            jax.ShapeDtypeStruct((hid, hid), BF),
            jax.ShapeDtypeStruct((104, hid), BF),
        ],
        scratch_shapes=[pltpu.VMEM(state.shape, BF), pltpu.VMEM(mask.shape, I32)]
        + [pltpu.VMEM(w.shape, BF) for w in weights]
        + [pltpu.VMEM((channels * cols, size), F32), pltpu.SemaphoreType.DMA((6,))],
        compiler_params=params(12),
        cost_estimate=pl.CostEstimate(flops=10**9, bytes_accessed=10**6, transcendentals=0),
        name="prepare",
    )(*in_hbm(state, mask, *weights))


def mlp_kernel(z0_ref, z1_ref, z2_ref, z3_ref, w1_ref, w2_ref, w3_ref, state_ref, *out_refs):
    z_refs, up_refs, send_ref = (z0_ref, z1_ref, z2_ref, z3_ref), out_refs[:4], out_refs[4]
    size, cols = z0_ref.shape
    rows = 4 * size
    step = 1024
    w1, w2, w3 = w1_ref[...], w2_ref[...], w3_ref[...]
    for c in range(0, cols, step):
        z = jnp.concatenate([ref[:, c : c + step].astype(F32) for ref in z_refs], axis=0)
        first = gelu(dot(w1, z.astype(BF))).astype(BF)
        second = gelu(dot(w2, first)).astype(BF)
        out = dot(w3, second)
        for k in range(4):
            span = slice(size * k, size * k + size)
            up = z[span] + out[span]
            if k == 1 or k == 3:
                rim = []
                for x in range(c // 128, (c + step) // 128):
                    tile = state_ref[x, 0:16] if k == 1 else state_ref[x, 112:128]
                    rim.append(tile.astype(F32)[:8] if k == 1 else tile.astype(F32)[8:])
                up = jnp.concatenate([up, jnp.concatenate(rim, axis=1)], axis=0)
            up_refs[k][:, c : c + step] = up.astype(BF)
        for k in range(0, step, 256):
            both = jnp.concatenate([out[rows : rows + 8, k : k + 128], out[rows : rows + 8, k + 128 : k + 256]], axis=0)
            send_ref[0, (c + k) // 256] = both.astype(BF)
    row, col = iota((48, 256), 0), iota((48, 256), 1)
    pick = (col == row // 3 * 16 + 13 + row % 3).astype(BF)
    strip = dot(pick, state_ref[:, 112:128].reshape(256, 128)).astype(BF)
    send_ref[0, 8:11] = strip.reshape(3, 16, 128)
    for j in range(1, send_ref.shape[0]):
        send_ref[j] = send_ref[0]


def column_model(pieces, w1, w2, w3, state):
    size, cols = pieces[0].shape
    return pl.pallas_call(
        mlp_kernel,
        in_specs=vmem_specs(8),
        out_specs=vmem_specs(5),
        out_shape=[
            jax.ShapeDtypeStruct((size, cols), BF),
            jax.ShapeDtypeStruct((size + 8, cols), BF),
            jax.ShapeDtypeStruct((size, cols), BF),
            jax.ShapeDtypeStruct((size + 8, cols), BF),
            jax.ShapeDtypeStruct((8, 11, 16, 128), BF),
        ],
        compiler_params=params(20),
        cost_estimate=pl.CostEstimate(flops=3 * 10**9, bytes_accessed=2 * 10**6, transcendentals=0),
        name="column_model",
    )(*pieces, w1, w2, w3, state)


def pack_kernel(seam_ref, near_ref, far_ref, got_ref, send_ref):
    tile, z_me = place()
    number, zs = [], []
    for m in range(ZS):
        ask = (near_ref if m < 4 else far_ref)[m % 4].astype(F32).astype(I32)
        for p in range(4):
            number.append(jnp.broadcast_to(ask[p : p + 1], (8, 128)))
            zs.append(jnp.broadcast_to(ask[4 + p : 5 + p], (8, 128)))
    number, zs = jnp.concatenate(number, axis=0), jnp.concatenate(zs, axis=0)
    wanted = jnp.where(zs == z_me, number * 8 + iota((256, 128), 0) % 8, -1)
    pick = [(wanted == iota((256, 128), 1) + 128 * j).astype(BF) for j in range(8)]
    blocks = jnp.concatenate([got_ref[j, 0:8].reshape(128, 128) for j in range(8)], axis=0)
    total = dot(jnp.concatenate(pick, axis=1), blocks)
    total = total.astype(BF).reshape(ZS, 2, 16, 128)
    for m in range(ZS):
        send_ref[ZS - 1 - (z_me ^ m), 0:2] = total[m]
    key = (seam_ref[0] + HALO) // 16 - 1 + 128
    core = lax.rem(tile, CS)
    z_to = lax.rem(key - lax.rem(key - core, CS) - CS * z_me, CS * ZS) // CS
    source = lax.rem(key - (tile - CS * z_me + CS * z_to), 64)
    strip = got_ref[source // (CS * ZS) * CS + lax.rem(source, CS), 8:11]
    for z in range(ZS):
        send_ref[z, 2:5] = strip


def pack(seam, near, far, got):
    return pl.pallas_call(
        pack_kernel,
        in_specs=[smem_spec()] + vmem_specs(3),
        out_specs=vmem_specs(1)[0],
        out_shape=jax.ShapeDtypeStruct((ZS, 5, 16, 128), BF),
        compiler_params=params(8),
        cost_estimate=pl.CostEstimate(flops=10**8, bytes_accessed=10**6, transcendentals=0),
        name="pack",
    )(seam, near, far, got)


def tall(state_ref, south_ref, north_ref, x):
    size = south_ref.shape[0] - 8
    lanes = slice(LANES * x, LANES * x + LANES)
    south = jnp.where(lax.axis_index("lev") > 0, south_ref[:, lanes].astype(F32)[size:], 0.0)
    return jnp.concatenate([south, state_ref[x].astype(F32), north_ref[:, lanes].astype(F32)[size:]], axis=0)


def remap_kernel(
    seam_ref, got_ref, margin_ref, state_ref, south_ref, north_ref,
    flux_ref, east_ref, west_ref, top_ref, strip_ref,
):
    partner = lax.rem((seam_ref[0] + HALO) // 16 - 1 - lax.axis_index("tile") + 128, 64)
    strip = got_ref[ZS - 1 - lax.rem(partner // CS, ZS), 2:5]
    strip_ref[...] = strip
    for side_ref, x in ((east_ref, 13), (west_ref, 0)):
        for k in range(HALO):
            side_ref[PITCH * k : PITCH * k + PITCH] = tall(state_ref, south_ref, north_ref, x + k).astype(BF)
        side_ref[432:480] = strip.reshape(48, 128)
    count = seam_ref[5]
    pieces = []
    for p in range(4):
        source = jnp.clip(seam_ref[1 + p], 0, 63)
        piece = got_ref[ZS - 1 - lax.rem(source // CS, ZS), p // 2].astype(F32)[8 * (p % 2) : 8 * (p % 2) + 8]
        pieces.append(jnp.where(p < count, piece, 0.0))
    blocks = jnp.concatenate(pieces, axis=0).astype(BF)
    spread = (iota((128, 2048), 0) == iota((128, 2048), 1) // 16).astype(BF)
    wide = dot(blocks, spread)
    same = iota((16, 2048), 0) == iota((16, 2048), 1) % 16
    total = None
    for p in range(4):
        rows = jnp.broadcast_to(wide[8 * p : 8 * p + 8][None], (16, 8, 2048))
        rows = jnp.where(same[:, None, :], rows, 0.0).reshape(128, 2048)
        ones = jnp.where(same & (p < count), 1.0, 0.0)
        left = jnp.concatenate([rows, ones], axis=0).astype(BF)
        term = dot(left, margin_ref[2048 * p : 2048 * p + 2048])
        total = term if total is None else total + term
    numer = total[:128].reshape(16, 8, 128)
    flux = (numer / total[128:144][:, None, :]).reshape(128, 128).astype(BF)
    flux_ref[...] = flux
    wide = flux.astype(F32)
    zero = jnp.zeros((8, 128), F32)
    east_ref[480:512] = jnp.concatenate([wide[104:128], zero], axis=0).astype(BF)
    west_ref[480:512] = jnp.concatenate([wide[0:24], zero], axis=0).astype(BF)
    top = dot_nt((iota((8, 128), 1) == 127 - iota((8, 128), 0)).astype(BF), flux).astype(BF)
    top_ref[...] = jnp.broadcast_to(top[None], top_ref.shape)


def remap(seam, got, margin, state, south, north, tiles):
    side = jax.ShapeDtypeStruct((512, 128), BF)
    return pl.pallas_call(
        remap_kernel,
        in_specs=[smem_spec()] + vmem_specs(5),
        out_specs=vmem_specs(5),
        out_shape=[
            jax.ShapeDtypeStruct((128, 128), BF),
            side,
            side,
            jax.ShapeDtypeStruct((tiles, 8, 128), BF),
            jax.ShapeDtypeStruct((3, 16, 128), BF),
        ],
        compiler_params=params(16),
        cost_estimate=pl.CostEstimate(flops=10**9, bytes_accessed=3 * 10**6, transcendentals=0),
        name="remap",
    )(seam, got, margin, state, south, north)


def rim_kernel(low_ref, flux_ref, high_ref, wide_ref, up_ref, down_ref):
    low, high = low_ref[480:512].astype(F32)[:24], high_ref[480:512].astype(F32)[:24]
    wide = jnp.concatenate([low, flux_ref[...].astype(F32), high, jnp.zeros((80, 128), F32)], axis=0).astype(BF)
    wide_ref[...] = wide
    row, col = iota((16, 128), 0), iota((16, 128), 1)
    up_ref[...] = dot_nt(((col == 125 + row) & (row < 3)).astype(BF), wide).astype(BF)
    down_ref[...] = dot_nt(((col == row) & (row < 3)).astype(BF), wide).astype(BF)


def rim(low, flux, high):
    strip = jax.ShapeDtypeStruct((16, 256), BF)
    return pl.pallas_call(
        rim_kernel,
        in_specs=vmem_specs(3),
        out_specs=vmem_specs(3),
        out_shape=[jax.ShapeDtypeStruct((256, 128), BF), strip, strip],
        compiler_params=params(4),
        cost_estimate=pl.CostEstimate(flops=10**8, bytes_accessed=10**6, transcendentals=0),
        name="rim",
    )(low, flux, high)


def conv_kernel(
    seam_ref, state_ref, below_ref, above_ref, west_ref, east_ref, strip_ref, wide_ref, south_ref, north_ref, tops_ref,
    w1_ref, w1r_ref, w3_ref, wmid_in, out_ref, v3, h3, h2, result, masks, w2_ref, sems,
):
    copies = fetch([(wmid_in, w2_ref)], sems)
    tiles = tops_ref.shape[0]
    tile = lax.axis_index("tile")
    top = lax.axis_index("lev") == lax.axis_size("lev") - 1
    n0, n1, n2, n3 = 22, 20, 18, 16
    seam = (seam_ref[0] + HALO) // 16
    shift = lax.rem(seam_ref[0] + HALO, 16)

    u, f = iota((128, 256), 0) // 8, iota((128, 256), 0) % 8
    i, g = iota((128, 256), 1) // 8, iota((128, 256), 1) % 8
    fold = None
    for e in range(3):
        pick = ((f == g) & (u == 16 * e + shift - i)).astype(BF)
        part = tops_ref[tiles - 1 - lax.rem(seam - tile - e + 2 * tiles, tiles)].astype(F32)
        term = dot(jnp.concatenate([part, jnp.zeros((8, 128), F32)], axis=0).astype(BF), pick)
        fold = term if fold is None else fold + term
    strips = jnp.concatenate(
        [west_ref[432:480], strip_ref[...].reshape(48, 128), east_ref[432:480]], axis=0
    )
    i, k = iota((352, 144), 0) // 16, iota((352, 144), 0) % 16 - 8
    e, u, r = iota((352, 144), 1) // 48, iota((352, 144), 1) % 48 // 3, iota((352, 144), 1) % 3
    folded = dot(((u == 16 * e + shift - i) & (r == 2 - k) & (k >= 0) & (k < 3)).astype(BF), strips)
    over = iota((16, LANES), 0)
    over = top & (over >= 8) & (over < 11)

    def state_of(x):
        if x < 3:
            v = west_ref[PITCH * x : PITCH * x + PITCH].astype(F32)
        elif x < 19:
            v = tall(state_ref, below_ref, above_ref, x - 3)
        else:
            v = east_ref[PITCH * (x - 19) : PITCH * (x - 19) + PITCH].astype(F32)
        return jnp.concatenate([v[:128], jnp.where(over, folded[16 * x : 16 * x + 16], v[128:])], axis=0)

    north = jnp.where(top, fold, north_ref[...].astype(F32))
    rims = jnp.concatenate([south_ref[...].astype(F32), north], axis=0).astype(BF)
    row, col = iota((PITCH, 128), 0), iota((PITCH, 128), 1)
    fluxes = dot_nt((row == col + 8).astype(BF), wide_ref[...])
    row, col = iota((PITCH, 32), 0), iota((PITCH, 32), 1)
    put = ((col < 3) & (row == col + 5)) | ((col >= 16) & (col < 19) & (row == col - 16 + 136))
    fluxes = fluxes + dot(put.astype(BF), rims)
    lane = iota((PITCH, LANES), 1)

    for x in range(n0):
        start = 8 * x
        part = fluxes[:, 128 * (start // 128) : 128 * (start // 128) + 128]
        part = pltpu.roll(part, (76 - start) % 128, 1)
        state = state_of(x)
        masks[x] = jnp.broadcast_to(state[:, 84:85], (PITCH, 128))
        v = jnp.where(lane < 76, state, jnp.where(lane < 84, part, 0.0))
        before = pltpu.roll(v, 1, 0)
        here = pltpu.roll(v, 84, 1)
        after = pltpu.roll(pltpu.roll(v, PITCH - 1, 0), 40, 1)
        v3[x, :, 0:128] = jnp.where(lane < 84, before, here).astype(BF)
        v3[x, :, 128:256] = jnp.where(lane < 40, here, after).astype(BF)

    def mask_of(x, lo, size):
        m = masks[x, lo : lo + size]
        return jnp.concatenate([m, m], axis=1)

    chunk = 4
    for c0 in range(0, n1, chunk):
        left = jnp.concatenate([v3[c0 + a : c0 + a + chunk].reshape(chunk * PITCH, 256) for a in range(3)], axis=1)
        acc = dot(left, w1_ref[...].reshape(768, 256))
        acc = acc.reshape(chunk, PITCH, 256)
        for k in range(chunk):
            x = c0 + k
            g = gelu(acc[k]) * mask_of(x + 1, 0, PITCH)
            h3[x, :, 0:256] = pltpu.roll(g, 1, 0).astype(BF)
            h3[x, :, 256:512] = g.astype(BF)
            h3[x, :, 512:768] = pltpu.roll(g, PITCH - 1, 0).astype(BF)

    @pl.when(top)
    def _():
        acc = None
        for a in range(3):
            d = dot(v3[a : a + n1, 128:144, :].reshape(n1 * 16, 256), w1r_ref[a])
            acc = d if acc is None else acc + d
        acc = acc.reshape(n1, 16, 256)
        row = iota((16, 256), 0)
        for x in range(n1):
            g = gelu(acc[x]) * mask_of(x + 1, 128, 16)
            old = h3[x, 128:144, 256:512].astype(F32)
            new = jnp.where((row == 8) | (row == 9), g, old)
            h3[x, 128:144, 256:512] = new.astype(BF)
            old = h3[x, 128:144, 0:256].astype(F32)
            h3[x, 128:144, 0:256] = jnp.where((row == 9) | (row == 10), pltpu.roll(new, 1, 0), old).astype(BF)
            old = h3[x, 128:144, 512:768].astype(F32)
            h3[x, 128:144, 512:768] = jnp.where((row == 7) | (row == 8), pltpu.roll(new, 15, 0), old).astype(BF)

    copies[0].wait()
    chunk = 2
    for c0 in range(0, n2, chunk):
        left = jnp.concatenate([h3[c0 + a : c0 + a + chunk].reshape(chunk * PITCH, 768) for a in range(3)], axis=1)
        acc = dot(left, w2_ref[...].reshape(2304, 256))
        acc = acc.reshape(chunk, PITCH, 256)
        for k in range(chunk):
            x = c0 + k
            h2[x] = (gelu(acc[k]) * mask_of(x + 2, 0, PITCH)).astype(BF)

    @pl.when(top)
    def _():
        acc = None
        for a in range(3):
            for b in range(3):
                lhs = h3[a : a + n2, 128:144, 256 * b : 256 * b + 256].reshape(n2 * 16, 256)
                d = dot(lhs, w2_ref[2 - a, 256 * (2 - b) : 256 * (2 - b) + 256, :])
                acc = d if acc is None else acc + d
        acc = acc.reshape(n2, 16, 256)
        row = iota((16, 256), 0)
        for x in range(n2):
            g = gelu(acc[x]) * mask_of(x + 2, 128, 16)
            old = h2[x, 128:144].astype(F32)
            h2[x, 128:144] = jnp.where(row == 8, g, old).astype(BF)

    chunk = 2
    for c0 in range(0, n3, chunk):
        left = jnp.concatenate([h2[c0 + a : c0 + a + chunk].reshape(chunk * PITCH, 256) for a in range(3)], axis=1)
        acc = dot_nt(left, w3_ref[...])
        acc = acc.reshape(chunk, PITCH, 384)
        for k in range(chunk):
            x = c0 + k
            change = (
                pltpu.roll(acc[k][:, 0:128], 1, 0)
                + acc[k][:, 128:256]
                + pltpu.roll(acc[k][:, 256:384], PITCH - 1, 0)
            )[8:136]
            new = (state_ref[x].astype(F32) + change) * masks[x + 3, 8:136]
            result[:, x, :] = new.T[:80]
    out_ref[...] = result[...][:76].astype(BF)


def weights_kernel(flux_ref, win_in, wout_in, w1_ref, w1r_ref, w3_ref, win_ref, wout_ref, sems):
    copies = fetch([(win_in, win_ref), (wout_in, wout_ref)], sems)
    copies[0].wait()
    for ref, turn in ((w1_ref, False), (w1r_ref, True)):
        for a in range(3):
            total = None
            for b in range(3):
                w = win_ref[2 - a, 2 - b] if turn else win_ref[a, b]
                term = dot((iota((256, 84), 0) == iota((256, 84), 1) + 84 * b).astype(BF), w)
                total = term if total is None else total + term
            ref[a] = total.astype(BF)
    copies[1].wait()
    for a in range(3):
        for b in range(3):
            w = wout_ref[a, b].astype(F32)
            w = jnp.concatenate([w, jnp.zeros((52, 256), F32)], axis=0).astype(BF)
            w3_ref[128 * b : 128 * b + 128, 256 * a : 256 * a + 256] = w


def conv_weights(flux, win, wout):
    return pl.pallas_call(
        weights_kernel,
        in_specs=vmem_specs(1) + hbm_specs(2),
        out_specs=vmem_specs(3),
        out_shape=[
            jax.ShapeDtypeStruct((3, 256, 256), BF),
            jax.ShapeDtypeStruct((3, 256, 256), BF),
            jax.ShapeDtypeStruct((384, 768), BF),
        ],
        scratch_shapes=[pltpu.VMEM(w.shape, BF) for w in (win, wout)] + [pltpu.SemaphoreType.DMA((2,))],
        compiler_params=params(8),
        cost_estimate=pl.CostEstimate(flops=10**9, bytes_accessed=4 * 10**6, transcendentals=0),
        name="conv_weights",
    )(flux, *in_hbm(win, wout))


def convolutions(*args):
    return pl.pallas_call(
        conv_kernel,
        in_specs=[smem_spec()] + vmem_specs(len(args) - 2) + hbm_specs(1),
        out_specs=vmem_specs(1)[0],
        out_shape=jax.ShapeDtypeStruct((76, 16, 128), BF),
        scratch_shapes=[
            pltpu.VMEM((22, PITCH, 256), BF),
            pltpu.VMEM((20, PITCH, 768), BF),
            pltpu.VMEM((18, PITCH, 256), BF),
            pltpu.VMEM((80, 16, 128), F32),
            pltpu.VMEM((22, PITCH, 128), F32),
        ]
        + [pltpu.VMEM(args[-1].shape, BF), pltpu.SemaphoreType.DMA((1,))],
        compiler_params=params(24),
        cost_estimate=pl.CostEstimate(flops=8 * 10**9, bytes_accessed=8 * 10**6, transcendentals=0),
        name="convolutions",
    )(*args[:-1], *in_hbm(args[-1]))


def shifted(forth, back, axis, periodic):
    count = lax.axis_size(axis)
    forward = [(i, i + 1) for i in range(count - 1)]
    if periodic:
        forward.append((count - 1, 0))
    backward = [(b, a) for a, b in forward]
    return lax.ppermute(forth, axis, forward), lax.ppermute(back, axis, backward)


def turned(x, axis, by):
    count = lax.axis_size(axis)
    return lax.ppermute(x, axis, [(i, (i + by) % count) for i in range(count)])


def per_tile(x, groups=None):
    return lax.all_to_all(x, "tile", split_axis=0, concat_axis=0, tiled=True, axis_index_groups=groups)


def per_device(
    atm_state,
    surface,
    mlp_in,
    mlp_mid,
    mlp_out,
    mlp_flux,
    ocean_state,
    ocean_mask,
    fold_map,
    pair_tile,
    pair_block,
    pair_count,
    margin,
    conv_in,
    conv_mid,
    conv_out,
):
    lev_dev = atm_state.shape[0]
    groups = lax.axis_size("lev")
    tiles = lax.axis_size("tile")
    _, span_x, span_y = ocean_state.shape
    pairs, blk = margin.shape[0], margin.shape[1]
    along_z = [[(x * ZS + z) * CS + c for z in reversed(range(ZS))] for x in range(tiles // (ZS * CS)) for c in range(CS)]
    same_z = [[(x * ZS + z) * CS + c for x in range(tiles // (ZS * CS)) for c in range(CS)] for z in range(ZS)]

    *pieces, asks, seam = collect(pair_count, pair_tile, pair_block, fold_map, atm_state, surface, groups)
    *pieces, asks, state_in = lax.optimization_barrier((*pieces, asks, ocean_state))
    pieces = [pieces[0]] + [turned(pieces[k], "lev", k) for k in range(1, groups)]

    def across(asks, bit):
        return lax.ppermute(asks, "tile", [(t, t ^ (CS * bit)) for t in range(tiles)])

    asks = jnp.concatenate([asks, across(asks, 1)], axis=0)

    state, *weights = prepare(state_in, ocean_mask, mlp_in, mlp_mid, mlp_out.T, mlp_flux.T)

    state, asks = lax.optimization_barrier((state, asks))
    *updated, send = column_model(pieces, *weights, state)
    send, second = lax.optimization_barrier((send, across(asks, 2)))
    near = jnp.concatenate([asks, second], axis=0)
    blocks = per_tile(send, same_z)
    got = per_tile(pack(seam, near, across(near, 4), blocks), along_z)

    back = [updated[0]] + [turned(updated[k], "lev", -k) for k in range(1, groups)]
    atm_next = spread(back, lev_dev)
    above, below = back[1], back[3]

    flux, last, first, top, partner = remap(
        seam, got, margin.reshape(pairs * blk * span_x, span_y), state, below, above, tiles
    )

    low, high = shifted(last, first, "tile", True)
    tops = per_tile(top, [list(reversed(range(tiles)))])
    conv_ws = conv_weights(last, conv_in, conv_out.transpose(0, 1, 3, 2))
    low, high, *conv_ws = lax.optimization_barrier((low, high, *conv_ws))
    wide, up, down = rim(low, flux, high)
    south, north = shifted(up, down, "lev", False)
    ocean_next = convolutions(
        seam, state, below, above, low, high, partner, wide, south, north, tops,
        *conv_ws, conv_mid.reshape(3, 768, 256),
    )
    return (atm_next, ocean_next)


def solution(mesh):
    return jax.shard_map(
        per_device,
        mesh=mesh,
        in_specs=(
            P("lev", None, "tile"),
            P("lev", "tile"),
            P(),
            P(),
            P(),
            P(),
            P(None, "tile", "lev"),
            P("tile", "lev"),
            P(),
            P("tile", "lev", None),
            P("tile", "lev", None),
            P("tile", "lev"),
            P(None, None, "tile", "lev"),
            P(),
            P(),
            P(),
        ),
        out_specs=(P("lev", None, "tile"), P(None, "tile", "lev")),
        check_vma=False,
    )
```

```python
import jax
import jax.numpy as jnp
from jax import lax
from jax.experimental import pallas as pl
from jax.experimental.pallas import tpu as pltpu
from jax.sharding import PartitionSpec as P

BF = jnp.bfloat16
F32 = jnp.float32
I32 = jnp.int32
SLAB = 8
HALO = 3
ZS, CS = 8, 2
PITCH = 144
LANES = 128
MIB = 1024 * 1024
C1 = 0.7978845608028654
C2 = C1 * 0.044715


def gelu(x):
    half = 0.5 * x
    return half * jnp.tanh(x * (C1 + C2 * (x * x))) + half


def dot(a, b):
    return jnp.dot(a, b, preferred_element_type=F32)


def dot_nt(a, b):
    return lax.dot_general(a, b, (((1,), (1,)), ((), ())), preferred_element_type=F32)


def iota(shape, dim):
    return lax.broadcasted_iota(I32, shape, dim)


def vmem_specs(n):
    return [pl.BlockSpec(memory_space=pltpu.VMEM)] * n


def hbm_specs(n):
    return [pl.BlockSpec(memory_space=pltpu.HBM)] * n


def in_hbm(*arrays):
    return [pltpu.with_memory_space_constraint(x, pltpu.HBM) for x in arrays]


def fetch(pairs, sems):
    copies = [pltpu.make_async_copy(a, b, sems.at[i]) for i, (a, b) in enumerate(pairs)]
    for copy in copies:
        copy.start()
    return copies


def smem_spec():
    return pl.BlockSpec(memory_space=pltpu.SMEM)


def params(mib):
    return pltpu.CompilerParams(vmem_limit_bytes=mib * MIB)


def place():
    tile = lax.axis_index("tile")
    return tile, lax.rem(tile // CS, ZS)


def collect_kernel(count_ref, tile_in, block_in, fold_in, atm_ref, surface_ref, *refs):
    *out_refs, ask_ref, seam_ref, tile_ref, block_ref, fold_ref, atm, surface, sems = refs
    levels, _, cols = atm_ref.shape
    parts = len(out_refs)
    size = cols // parts
    lev = lax.axis_index("lev")
    zero = jnp.zeros((1, size), F32)
    spans = [pl.ds(pl.multiple_of(lax.rem(lev + k, parts) * size, size), size) for k in range(parts)]
    order = (1, 2, 3, 0)
    tables = [(tile_in, tile_ref), (block_in, block_ref), (fold_in, fold_ref)]
    copies = fetch(
        tables + [(surface_ref, surface)] + [(atm_ref.at[:, :, spans[k]], atm.at[k]) for k in order], sems
    )
    for copy in copies[:3]:
        copy.wait()
    seam_ref[0] = fold_ref[0]
    seam_ref[5] = count_ref[0, 0]
    rows, zs = [], []
    for p in range(4):
        source, block = tile_ref[0, 0, p], block_ref[0, 0, p]
        seam_ref[1 + p] = source
        number = (source // (CS * ZS) * CS + lax.rem(source, CS)) * 16 + block
        z = jnp.where(p < count_ref[0, 0], lax.rem(source // CS, ZS), -1)
        rows.append(jnp.full((1, 128), number, I32))
        zs.append(jnp.full((1, 128), z, I32))
    ask_ref[0] = jnp.concatenate(rows + zs + [jnp.zeros((8, 128), I32)], axis=0).astype(F32).astype(BF)
    copies[3].wait()
    for i, k in enumerate(order):
        copies[4 + i].wait()
        rows = []
        for j in range(levels):
            extra = surface[:, spans[k]].astype(F32) if j == 0 else zero
            rows += [atm[k, j].astype(F32), extra, zero]
        out_refs[k][...] = jnp.concatenate(rows, axis=0).astype(BF)


def collect(count, tile, block, fold_map, atm, surface, parts):
    levels, _, cols = atm.shape
    return pl.pallas_call(
        collect_kernel,
        in_specs=[smem_spec()] + hbm_specs(5),
        out_specs=vmem_specs(parts + 1) + [smem_spec()],
        out_shape=[jax.ShapeDtypeStruct((levels * SLAB, cols // parts), BF)] * parts
        + [jax.ShapeDtypeStruct((1, 16, 128), BF), jax.ShapeDtypeStruct((8,), I32)],
        scratch_shapes=[pltpu.SMEM(x.shape, I32) for x in (tile, block, fold_map)]
        + [
            pltpu.VMEM((parts, levels, 6, cols // parts), BF),
            pltpu.VMEM((1, cols), BF),
            pltpu.SemaphoreType.DMA((parts + 4,)),
        ],
        compiler_params=params(8),
        cost_estimate=pl.CostEstimate(flops=10**6, bytes_accessed=10**6, transcendentals=0),
        name="collect",
    )(count, *in_hbm(tile, block, fold_map, atm, surface))


def spread_kernel(*refs):
    back_refs, out_ref = refs[:-1], refs[-1]
    parts, size = len(back_refs), back_refs[0].shape[1]
    lev = lax.axis_index("lev")
    for k in range(parts):
        rows = back_refs[k][...].astype(F32)
        span = pl.ds(pl.multiple_of(lax.rem(lev + k, parts) * size, size), size)
        for j in range(out_ref.shape[0]):
            out_ref[j, :, span] = rows[SLAB * j : SLAB * j + 6].astype(BF)


def spread(back, levels):
    parts, size = len(back), back[0].shape[1]
    return pl.pallas_call(
        spread_kernel,
        in_specs=vmem_specs(parts),
        out_specs=vmem_specs(1)[0],
        out_shape=jax.ShapeDtypeStruct((levels, 6, parts * size), BF),
        compiler_params=params(8),
        cost_estimate=pl.CostEstimate(flops=10**6, bytes_accessed=10**6, transcendentals=0),
        name="spread",
    )(*back)


def prepare_kernel(
    state_in, mask_in, win_in, wmid_in, wout_in, wflux_in, state_ref, w1_ref, w2_ref, w3_ref,
    state, mask_ref, win_ref, wmid_ref, wout_ref, wflux_ref, rows, sems,
):
    copies = fetch(
        [
            (state_in, state), (mask_in, mask_ref), (win_in, win_ref), (wmid_in, wmid_ref), (wout_in, wout_ref),
            (wflux_in, wflux_ref),
        ],
        sems,
    )
    channels, cols, size = state_in.shape
    copies[0].wait()
    copies[1].wait()
    rows[...] = state[...].reshape(channels * cols, size).astype(F32)
    for x in range(cols):
        part = rows[pl.ds(x, channels, stride=cols), :]
        mask = mask_ref[x : x + 1].astype(F32)
        part = jnp.concatenate(
            [part, jnp.zeros((84 - channels, size), F32), mask, jnp.zeros((LANES - 85, size), F32)], axis=0
        )
        state_ref[x] = part.T.astype(BF)
    for copy in copies[2:]:
        copy.wait()
    lev = lax.axis_index("lev")
    rows_all = w1_ref.shape[1]
    size = rows_all // 4

    def origin(shape):
        row = iota(shape, 0)
        group = (lev - row // size) & 3
        level, field = 3 * group + row % size // 8, row % 8
        return jnp.where((field < 6) & (row < rows_all), 6 * level + field, -1), group, row

    source, group, row = origin((rows_all, 76))
    source = jnp.where(row % size == 6, 72 + group, source)
    w1_ref[...] = dot((iota((rows_all, 76), 1) == source).astype(BF), win_ref[...]).T.astype(BF)
    source, group, row = origin((rows_all + 8, 72))
    w3 = dot((iota((rows_all + 8, 72), 1) == source).astype(BF), wout_ref[...])
    w3 = w3 + dot((iota((rows_all + 8, 8), 1) == iota((rows_all + 8, 8), 0) - rows_all).astype(BF), wflux_ref[...])
    w3_ref[...] = w3.astype(BF)
    w2_ref[...] = wmid_ref[...].T


def prepare(state, mask, *weights):
    channels, cols, size = state.shape
    hid = weights[1].shape[0]
    return pl.pallas_call(
        prepare_kernel,
        in_specs=hbm_specs(6),
        out_specs=vmem_specs(4),
        out_shape=[
            jax.ShapeDtypeStruct((cols, size, LANES), BF),
            jax.ShapeDtypeStruct((hid, 96), BF),
            jax.ShapeDtypeStruct((hid, hid), BF),
            jax.ShapeDtypeStruct((104, hid), BF),
        ],
        scratch_shapes=[pltpu.VMEM(state.shape, BF), pltpu.VMEM(mask.shape, I32)]
        + [pltpu.VMEM(w.shape, BF) for w in weights]
        + [pltpu.VMEM((channels * cols, size), F32), pltpu.SemaphoreType.DMA((6,))],
        compiler_params=params(12),
        cost_estimate=pl.CostEstimate(flops=10**9, bytes_accessed=10**6, transcendentals=0),
        name="prepare",
    )(*in_hbm(state, mask, *weights))


def mlp_kernel(z0_ref, z1_ref, z2_ref, z3_ref, w1_ref, w2_ref, w3_ref, state_ref, *out_refs):
    z_refs, up_refs, send_ref = (z0_ref, z1_ref, z2_ref, z3_ref), out_refs[:4], out_refs[4]
    size, cols = z0_ref.shape
    rows = 4 * size
    step = 1024
    w1, w2, w3 = w1_ref[...], w2_ref[...], w3_ref[...]
    for c in range(0, cols, step):
        z = jnp.concatenate([ref[:, c : c + step].astype(F32) for ref in z_refs], axis=0)
        first = gelu(dot(w1, z.astype(BF))).astype(BF)
        second = gelu(dot(w2, first)).astype(BF)
        out = dot(w3, second)
        for k in range(4):
            span = slice(size * k, size * k + size)
            up = z[span] + out[span]
            if k == 1 or k == 3:
                rim = []
                for x in range(c // 128, (c + step) // 128):
                    tile = state_ref[x, 0:16] if k == 1 else state_ref[x, 112:128]
                    rim.append(tile.astype(F32)[:8] if k == 1 else tile.astype(F32)[8:])
                up = jnp.concatenate([up, jnp.concatenate(rim, axis=1)], axis=0)
            up_refs[k][:, c : c + step] = up.astype(BF)
        for k in range(0, step, 256):
            both = jnp.concatenate([out[rows : rows + 8, k : k + 128], out[rows : rows + 8, k + 128 : k + 256]], axis=0)
            send_ref[0, (c + k) // 256] = both.astype(BF)
    row, col = iota((48, 256), 0), iota((48, 256), 1)
    pick = (col == row // 3 * 16 + 13 + row % 3).astype(BF)
    strip = dot(pick, state_ref[:, 112:128].reshape(256, 128)).astype(BF)
    send_ref[0, 8:11] = strip.reshape(3, 16, 128)
    for j in range(1, send_ref.shape[0]):
        send_ref[j] = send_ref[0]


def column_model(pieces, w1, w2, w3, state):
    size, cols = pieces[0].shape
    return pl.pallas_call(
        mlp_kernel,
        in_specs=vmem_specs(8),
        out_specs=vmem_specs(5),
        out_shape=[
            jax.ShapeDtypeStruct((size, cols), BF),
            jax.ShapeDtypeStruct((size + 8, cols), BF),
            jax.ShapeDtypeStruct((size, cols), BF),
            jax.ShapeDtypeStruct((size + 8, cols), BF),
            jax.ShapeDtypeStruct((8, 11, 16, 128), BF),
        ],
        compiler_params=params(20),
        cost_estimate=pl.CostEstimate(flops=3 * 10**9, bytes_accessed=2 * 10**6, transcendentals=0),
        name="column_model",
    )(*pieces, w1, w2, w3, state)


def pack_kernel(seam_ref, near_ref, far_ref, got_ref, send_ref):
    tile, z_me = place()
    number, zs = [], []
    for m in range(ZS):
        ask = (near_ref if m < 4 else far_ref)[m % 4].astype(F32).astype(I32)
        for p in range(4):
            number.append(jnp.broadcast_to(ask[p : p + 1], (8, 128)))
            zs.append(jnp.broadcast_to(ask[4 + p : 5 + p], (8, 128)))
    number, zs = jnp.concatenate(number, axis=0), jnp.concatenate(zs, axis=0)
    wanted = jnp.where(zs == z_me, number * 8 + iota((256, 128), 0) % 8, -1)
    pick = [(wanted == iota((256, 128), 1) + 128 * j).astype(BF) for j in range(8)]
    blocks = jnp.concatenate([got_ref[7 - j, 0:8].reshape(128, 128) for j in range(8)], axis=0)
    total = dot(jnp.concatenate(pick, axis=1), blocks)
    total = total.astype(BF).reshape(ZS, 2, 16, 128)
    for m in range(ZS):
        send_ref[ZS - 1 - (z_me ^ m), 0:2] = total[m]
    key = (seam_ref[0] + HALO) // 16 - 1 + 128
    core = lax.rem(tile, CS)
    z_to = lax.rem(key - lax.rem(key - core, CS) - CS * z_me, CS * ZS) // CS
    source = lax.rem(key - (tile - CS * z_me + CS * z_to), 64)
    strip = got_ref[7 - (source // (CS * ZS) * CS + lax.rem(source, CS)), 8:11]
    for z in range(ZS):
        send_ref[z, 2:5] = strip


def pack(seam, near, far, got):
    return pl.pallas_call(
        pack_kernel,
        in_specs=[smem_spec()] + vmem_specs(3),
        out_specs=vmem_specs(1)[0],
        out_shape=jax.ShapeDtypeStruct((ZS, 5, 16, 128), BF),
        compiler_params=params(8),
        cost_estimate=pl.CostEstimate(flops=10**8, bytes_accessed=10**6, transcendentals=0),
        name="pack",
    )(seam, near, far, got)


def tall(state_ref, south_ref, north_ref, x):
    size = south_ref.shape[0] - 8
    lanes = slice(LANES * x, LANES * x + LANES)
    south = jnp.where(lax.axis_index("lev") > 0, south_ref[:, lanes].astype(F32)[size:], 0.0)
    return jnp.concatenate([south, state_ref[x].astype(F32), north_ref[:, lanes].astype(F32)[size:]], axis=0)


def remap_kernel(
    seam_ref, got_ref, margin_ref, state_ref, south_ref, north_ref,
    flux_ref, east_ref, west_ref, top_ref, strip_ref,
):
    partner = lax.rem((seam_ref[0] + HALO) // 16 - 1 - lax.axis_index("tile") + 128, 64)
    strip = got_ref[ZS - 1 - lax.rem(partner // CS, ZS), 2:5]
    strip_ref[...] = strip
    for side_ref, x in ((east_ref, 13), (west_ref, 0)):
        for k in range(HALO):
            side_ref[PITCH * k : PITCH * k + PITCH] = tall(state_ref, south_ref, north_ref, x + k).astype(BF)
        side_ref[432:480] = strip.reshape(48, 128)
    count = seam_ref[5]
    pieces = []
    for p in range(4):
        source = jnp.clip(seam_ref[1 + p], 0, 63)
        piece = got_ref[ZS - 1 - lax.rem(source // CS, ZS), p // 2].astype(F32)[8 * (p % 2) : 8 * (p % 2) + 8]
        pieces.append(jnp.where(p < count, piece, 0.0))
    blocks = jnp.concatenate(pieces, axis=0).astype(BF)
    spread = (iota((128, 2048), 0) == iota((128, 2048), 1) // 16).astype(BF)
    wide = dot(blocks, spread)
    same = iota((16, 2048), 0) == iota((16, 2048), 1) % 16
    total = None
    for p in range(4):
        rows = jnp.broadcast_to(wide[8 * p : 8 * p + 8][None], (16, 8, 2048))
        rows = jnp.where(same[:, None, :], rows, 0.0).reshape(128, 2048)
        ones = jnp.where(same & (p < count), 1.0, 0.0)
        left = jnp.concatenate([rows, ones], axis=0).astype(BF)
        term = dot(left, margin_ref[2048 * p : 2048 * p + 2048])
        total = term if total is None else total + term
    numer = total[:128].reshape(16, 8, 128)
    flux = (numer / total[128:144][:, None, :]).reshape(128, 128).astype(BF)
    flux_ref[...] = flux
    wide = flux.astype(F32)
    zero = jnp.zeros((8, 128), F32)
    east_ref[480:512] = jnp.concatenate([wide[104:128], zero], axis=0).astype(BF)
    west_ref[480:512] = jnp.concatenate([wide[0:24], zero], axis=0).astype(BF)
    top = dot_nt((iota((8, 128), 1) == 127 - iota((8, 128), 0)).astype(BF), flux).astype(BF)
    top_ref[...] = jnp.broadcast_to(top[None], top_ref.shape)


def remap(seam, got, margin, state, south, north, tiles):
    side = jax.ShapeDtypeStruct((512, 128), BF)
    return pl.pallas_call(
        remap_kernel,
        in_specs=[smem_spec()] + vmem_specs(5),
        out_specs=vmem_specs(5),
        out_shape=[
            jax.ShapeDtypeStruct((128, 128), BF),
            side,
            side,
            jax.ShapeDtypeStruct((tiles, 8, 128), BF),
            jax.ShapeDtypeStruct((3, 16, 128), BF),
        ],
        compiler_params=params(16),
        cost_estimate=pl.CostEstimate(flops=10**9, bytes_accessed=3 * 10**6, transcendentals=0),
        name="remap",
    )(seam, got, margin, state, south, north)


def rim_kernel(low_ref, flux_ref, high_ref, wide_ref, up_ref, down_ref):
    low, high = low_ref[480:512].astype(F32)[:24], high_ref[480:512].astype(F32)[:24]
    wide = jnp.concatenate([low, flux_ref[...].astype(F32), high, jnp.zeros((80, 128), F32)], axis=0).astype(BF)
    wide_ref[...] = wide
    row, col = iota((16, 128), 0), iota((16, 128), 1)
    up_ref[...] = dot_nt(((col == 125 + row) & (row < 3)).astype(BF), wide).astype(BF)
    down_ref[...] = dot_nt(((col == row) & (row < 3)).astype(BF), wide).astype(BF)


def rim(low, flux, high):
    strip = jax.ShapeDtypeStruct((16, 256), BF)
    return pl.pallas_call(
        rim_kernel,
        in_specs=vmem_specs(3),
        out_specs=vmem_specs(3),
        out_shape=[jax.ShapeDtypeStruct((256, 128), BF), strip, strip],
        compiler_params=params(4),
        cost_estimate=pl.CostEstimate(flops=10**8, bytes_accessed=10**6, transcendentals=0),
        name="rim",
    )(low, flux, high)


def conv_kernel(
    seam_ref, state_ref, below_ref, above_ref, west_ref, east_ref, strip_ref, wide_ref, south_ref, north_ref, tops_ref,
    w1_ref, w1r_ref, w3_ref, wmid_in, out_ref, v3, h3, h2, result, masks, w2_ref, sems,
):
    copies = fetch([(wmid_in, w2_ref)], sems)
    tiles = tops_ref.shape[0]
    tile = lax.axis_index("tile")
    top = lax.axis_index("lev") == lax.axis_size("lev") - 1
    n0, n1, n2, n3 = 22, 20, 18, 16
    seam = (seam_ref[0] + HALO) // 16
    shift = lax.rem(seam_ref[0] + HALO, 16)

    u, f = iota((128, 256), 0) // 8, iota((128, 256), 0) % 8
    i, g = iota((128, 256), 1) // 8, iota((128, 256), 1) % 8
    fold = None
    for e in range(3):
        pick = ((f == g) & (u == 16 * e + shift - i)).astype(BF)
        part = tops_ref[tiles - 1 - lax.rem(seam - tile - e + 2 * tiles, tiles)].astype(F32)
        term = dot(jnp.concatenate([part, jnp.zeros((8, 128), F32)], axis=0).astype(BF), pick)
        fold = term if fold is None else fold + term
    strips = jnp.concatenate(
        [west_ref[432:480], strip_ref[...].reshape(48, 128), east_ref[432:480]], axis=0
    )
    i, k = iota((352, 144), 0) // 16, iota((352, 144), 0) % 16 - 8
    e, u, r = iota((352, 144), 1) // 48, iota((352, 144), 1) % 48 // 3, iota((352, 144), 1) % 3
    folded = dot(((u == 16 * e + shift - i) & (r == 2 - k) & (k >= 0) & (k < 3)).astype(BF), strips)
    over = iota((16, LANES), 0)
    over = top & (over >= 8) & (over < 11)

    def state_of(x):
        if x < 3:
            v = west_ref[PITCH * x : PITCH * x + PITCH].astype(F32)
        elif x < 19:
            v = tall(state_ref, below_ref, above_ref, x - 3)
        else:
            v = east_ref[PITCH * (x - 19) : PITCH * (x - 19) + PITCH].astype(F32)
        return jnp.concatenate([v[:128], jnp.where(over, folded[16 * x : 16 * x + 16], v[128:])], axis=0)

    north = jnp.where(top, fold, north_ref[...].astype(F32))
    rims = jnp.concatenate([south_ref[...].astype(F32), north], axis=0).astype(BF)
    row, col = iota((PITCH, 128), 0), iota((PITCH, 128), 1)
    fluxes = dot_nt((row == col + 8).astype(BF), wide_ref[...])
    row, col = iota((PITCH, 32), 0), iota((PITCH, 32), 1)
    put = ((col < 3) & (row == col + 5)) | ((col >= 16) & (col < 19) & (row == col - 16 + 136))
    fluxes = fluxes + dot(put.astype(BF), rims)
    lane = iota((PITCH, LANES), 1)

    for x in range(n0):
        start = 8 * x
        part = fluxes[:, 128 * (start // 128) : 128 * (start // 128) + 128]
        part = pltpu.roll(part, (76 - start) % 128, 1)
        state = state_of(x)
        masks[x] = jnp.broadcast_to(state[:, 84:85], (PITCH, 128))
        v = jnp.where(lane < 76, state, jnp.where(lane < 84, part, 0.0))
        before = pltpu.roll(v, 1, 0)
        here = pltpu.roll(v, 84, 1)
        after = pltpu.roll(pltpu.roll(v, PITCH - 1, 0), 40, 1)
        v3[x, :, 0:128] = jnp.where(lane < 84, before, here).astype(BF)
        v3[x, :, 128:256] = jnp.where(lane < 40, here, after).astype(BF)

    def mask_of(x, lo, size):
        m = masks[x, lo : lo + size]
        return jnp.concatenate([m, m], axis=1)

    chunk = 4
    for c0 in range(0, n1, chunk):
        left = jnp.concatenate([v3[c0 + a : c0 + a + chunk].reshape(chunk * PITCH, 256) for a in range(3)], axis=1)
        acc = dot(left, w1_ref[...].reshape(768, 256))
        acc = acc.reshape(chunk, PITCH, 256)
        for k in range(chunk):
            x = c0 + k
            g = gelu(acc[k]) * mask_of(x + 1, 0, PITCH)
            h3[x, :, 0:256] = pltpu.roll(g, 1, 0).astype(BF)
            h3[x, :, 256:512] = g.astype(BF)
            h3[x, :, 512:768] = pltpu.roll(g, PITCH - 1, 0).astype(BF)

    @pl.when(top)
    def _():
        acc = None
        for a in range(3):
            d = dot(v3[a : a + n1, 128:144, :].reshape(n1 * 16, 256), w1r_ref[a])
            acc = d if acc is None else acc + d
        acc = acc.reshape(n1, 16, 256)
        row = iota((16, 256), 0)
        for x in range(n1):
            g = gelu(acc[x]) * mask_of(x + 1, 128, 16)
            old = h3[x, 128:144, 256:512].astype(F32)
            new = jnp.where((row == 8) | (row == 9), g, old)
            h3[x, 128:144, 256:512] = new.astype(BF)
            old = h3[x, 128:144, 0:256].astype(F32)
            h3[x, 128:144, 0:256] = jnp.where((row == 9) | (row == 10), pltpu.roll(new, 1, 0), old).astype(BF)
            old = h3[x, 128:144, 512:768].astype(F32)
            h3[x, 128:144, 512:768] = jnp.where((row == 7) | (row == 8), pltpu.roll(new, 15, 0), old).astype(BF)

    copies[0].wait()
    chunk = 2
    for c0 in range(0, n2, chunk):
        left = jnp.concatenate([h3[c0 + a : c0 + a + chunk].reshape(chunk * PITCH, 768) for a in range(3)], axis=1)
        acc = dot(left, w2_ref[...].reshape(2304, 256))
        acc = acc.reshape(chunk, PITCH, 256)
        for k in range(chunk):
            x = c0 + k
            h2[x] = (gelu(acc[k]) * mask_of(x + 2, 0, PITCH)).astype(BF)

    @pl.when(top)
    def _():
        acc = None
        for a in range(3):
            for b in range(3):
                lhs = h3[a : a + n2, 128:144, 256 * b : 256 * b + 256].reshape(n2 * 16, 256)
                d = dot(lhs, w2_ref[2 - a, 256 * (2 - b) : 256 * (2 - b) + 256, :])
                acc = d if acc is None else acc + d
        acc = acc.reshape(n2, 16, 256)
        row = iota((16, 256), 0)
        for x in range(n2):
            g = gelu(acc[x]) * mask_of(x + 2, 128, 16)
            old = h2[x, 128:144].astype(F32)
            h2[x, 128:144] = jnp.where(row == 8, g, old).astype(BF)

    chunk = 2
    for c0 in range(0, n3, chunk):
        left = jnp.concatenate([h2[c0 + a : c0 + a + chunk].reshape(chunk * PITCH, 256) for a in range(3)], axis=1)
        acc = dot_nt(left, w3_ref[...])
        acc = acc.reshape(chunk, PITCH, 384)
        for k in range(chunk):
            x = c0 + k
            change = (
                pltpu.roll(acc[k][:, 0:128], 1, 0)
                + acc[k][:, 128:256]
                + pltpu.roll(acc[k][:, 256:384], PITCH - 1, 0)
            )[8:136]
            new = (state_ref[x].astype(F32) + change) * masks[x + 3, 8:136]
            result[:, x, :] = new.T[:80]
    out_ref[...] = result[...][:76].astype(BF)


def weights_kernel(flux_ref, win_in, wout_in, w1_ref, w1r_ref, w3_ref, win_ref, wout_ref, sems):
    copies = fetch([(win_in, win_ref), (wout_in, wout_ref)], sems)
    copies[0].wait()
    for ref, turn in ((w1_ref, False), (w1r_ref, True)):
        for a in range(3):
            total = None
            for b in range(3):
                w = win_ref[2 - a, 2 - b] if turn else win_ref[a, b]
                term = dot((iota((256, 84), 0) == iota((256, 84), 1) + 84 * b).astype(BF), w)
                total = term if total is None else total + term
            ref[a] = total.astype(BF)
    copies[1].wait()
    for a in range(3):
        for b in range(3):
            w = wout_ref[a, b].astype(F32)
            w = jnp.concatenate([w, jnp.zeros((52, 256), F32)], axis=0).astype(BF)
            w3_ref[128 * b : 128 * b + 128, 256 * a : 256 * a + 256] = w


def conv_weights(flux, win, wout):
    return pl.pallas_call(
        weights_kernel,
        in_specs=vmem_specs(1) + hbm_specs(2),
        out_specs=vmem_specs(3),
        out_shape=[
            jax.ShapeDtypeStruct((3, 256, 256), BF),
            jax.ShapeDtypeStruct((3, 256, 256), BF),
            jax.ShapeDtypeStruct((384, 768), BF),
        ],
        scratch_shapes=[pltpu.VMEM(w.shape, BF) for w in (win, wout)] + [pltpu.SemaphoreType.DMA((2,))],
        compiler_params=params(8),
        cost_estimate=pl.CostEstimate(flops=10**9, bytes_accessed=4 * 10**6, transcendentals=0),
        name="conv_weights",
    )(flux, *in_hbm(win, wout))


def convolutions(*args):
    return pl.pallas_call(
        conv_kernel,
        in_specs=[smem_spec()] + vmem_specs(len(args) - 2) + hbm_specs(1),
        out_specs=vmem_specs(1)[0],
        out_shape=jax.ShapeDtypeStruct((76, 16, 128), BF),
        scratch_shapes=[
            pltpu.VMEM((22, PITCH, 256), BF),
            pltpu.VMEM((20, PITCH, 768), BF),
            pltpu.VMEM((18, PITCH, 256), BF),
            pltpu.VMEM((80, 16, 128), F32),
            pltpu.VMEM((22, PITCH, 128), F32),
        ]
        + [pltpu.VMEM(args[-1].shape, BF), pltpu.SemaphoreType.DMA((1,))],
        compiler_params=params(24),
        cost_estimate=pl.CostEstimate(flops=8 * 10**9, bytes_accessed=8 * 10**6, transcendentals=0),
        name="convolutions",
    )(*args[:-1], *in_hbm(args[-1]))


def shifted(forth, back, axis, periodic):
    count = lax.axis_size(axis)
    forward = [(i, i + 1) for i in range(count - 1)]
    if periodic:
        forward.append((count - 1, 0))
    backward = [(b, a) for a, b in forward]
    return lax.ppermute(forth, axis, forward), lax.ppermute(back, axis, backward)


def turned(x, axis, by):
    count = lax.axis_size(axis)
    return lax.ppermute(x, axis, [(i, (i + by) % count) for i in range(count)])


def per_tile(x, groups=None):
    return lax.all_to_all(x, "tile", split_axis=0, concat_axis=0, tiled=True, axis_index_groups=groups)


def per_device(
    atm_state,
    surface,
    mlp_in,
    mlp_mid,
    mlp_out,
    mlp_flux,
    ocean_state,
    ocean_mask,
    fold_map,
    pair_tile,
    pair_block,
    pair_count,
    margin,
    conv_in,
    conv_mid,
    conv_out,
):
    lev_dev = atm_state.shape[0]
    groups = lax.axis_size("lev")
    tiles = lax.axis_size("tile")
    _, span_x, span_y = ocean_state.shape
    pairs, blk = margin.shape[0], margin.shape[1]
    along_z = [[(x * ZS + z) * CS + c for z in reversed(range(ZS))] for x in range(tiles // (ZS * CS)) for c in range(CS)]
    same_z = [[(x * ZS + z) * CS + c for x in range(tiles // (ZS * CS)) for c in range(CS)][::-1] for z in range(ZS)]

    *pieces, asks, seam = collect(pair_count, pair_tile, pair_block, fold_map, atm_state, surface, groups)
    *pieces, asks, state_in = lax.optimization_barrier((*pieces, asks, ocean_state))
    pieces = [pieces[0]] + [turned(pieces[k], "lev", k) for k in range(1, groups)]

    def across(asks, bit):
        return lax.ppermute(asks, "tile", [(t, t ^ (CS * bit)) for t in range(tiles)])

    asks = jnp.concatenate([asks, across(asks, 1)], axis=0)

    state, *weights = prepare(state_in, ocean_mask, mlp_in, mlp_mid, mlp_out.T, mlp_flux.T)

    state, asks = lax.optimization_barrier((state, asks))
    *updated, send = column_model(pieces, *weights, state)
    send, second = lax.optimization_barrier((send, across(asks, 2)))
    near = jnp.concatenate([asks, second], axis=0)
    blocks = per_tile(send, same_z)
    got = per_tile(pack(seam, near, across(near, 4), blocks), along_z)

    back = [updated[0]] + [turned(updated[k], "lev", -k) for k in range(1, groups)]
    atm_next = spread(back, lev_dev)
    above, below = back[1], back[3]

    flux, last, first, top, partner = remap(
        seam, got, margin.reshape(pairs * blk * span_x, span_y), state, below, above, tiles
    )

    low, high = shifted(last, first, "tile", True)
    tops = per_tile(top, [list(reversed(range(tiles)))])
    conv_ws = conv_weights(last, conv_in, conv_out.transpose(0, 1, 3, 2))
    low, high, *conv_ws = lax.optimization_barrier((low, high, *conv_ws))
    wide, up, down = rim(low, flux, high)
    south, north = shifted(up, down, "lev", False)
    ocean_next = convolutions(
        seam, state, below, above, low, high, partner, wide, south, north, tops,
        *conv_ws, conv_mid.reshape(3, 768, 256),
    )
    return (atm_next, ocean_next)


def solution(mesh):
    return jax.shard_map(
        per_device,
        mesh=mesh,
        in_specs=(
            P("lev", None, "tile"),
            P("lev", "tile"),
            P(),
            P(),
            P(),
            P(),
            P(None, "tile", "lev"),
            P("tile", "lev"),
            P(),
            P("tile", "lev", None),
            P("tile", "lev", None),
            P("tile", "lev"),
            P(None, None, "tile", "lev"),
            P(),
            P(),
            P(),
        ),
        out_specs=(P("lev", None, "tile"), P(None, "tile", "lev")),
        check_vma=False,
    )
```
